512 devices in a mesh: blk: 16 (over x, y_hi, core), dp: 32 (over z, y_lo).
Axes of the slice: x: 4, y: 4 (y_hi: 2, y_lo: 2; y = y_hi * 2 + y_lo), z: 16, core: 2. Of those that a mesh axis runs over, the one named last changes fastest.
Arguments:
- inputs: bfloat16 [65536, 5120], P(('blk', 'dp')), may hold values from -400 to 400
- queries: bfloat16 [65536, 2560], P(('blk', 'dp')), may hold values from -96 to 96
- keys: bfloat16 [65536, 512], P(('blk', 'dp')), may hold values from -4 to 4
- doc_ids: int32 [65536], P(('blk', 'dp')), may hold values from 0 to 65535, as said below
- grad_out: bfloat16 [65536, 2560], P(('blk', 'dp')), may hold values from -6 to 6
- gain: float32 [5120], replicated, may hold values from 0.25 to 1.75
- bias: float32 [512], replicated, may hold values from -3 to 3
- w_value: bfloat16 [5120, 512], P('blk'), may hold values from -0.078125 to 0.078125
Outputs:
- attention: bfloat16 [65536, 2560], P(('blk', 'dp'))
- grad_inputs: bfloat16 [65536, 5120], P(('blk', 'dp'))
- grad_w_value: float32 [5120, 512], P('blk', 'dp')
- grad_gain: float32 [5120], replicated
- grad_bias: float32 [512], replicated
The draws below stay inside these ranges and needn't reach their ends.
Inputs may be any that keep to these rules, and one draw needn't show every extreme that they name: `doc_ids`: document ids never fall along the tokens; the first token has id 0 and the last token alone has id 65536 - 1.
All inputs are finite; a program needn't handle non-finite values.
Results may differ from the reference program's by a relative error of at most 0.012.
Values may be sent and summed in bfloat16 or wider, within the bound.
A program may use at most 64 MiB of HBM per device.

```python
import math
import jax
import jax.numpy as jnp
from jax import lax

D = 5120
HD = 128
TOK_DEV = 128
QD = 2560
KVD = 512
TOKENS = 65536
N_DP = 32


def mark_starts(key):
    coin = jax.random.randint(jax.random.fold_in(key, 501), (TOKENS,), 0, 48)
    first = jnp.arange(TOKENS) == 0
    return (coin == 0) | first


def pick_rows(key):
    starts = mark_starts(key)
    coin = jax.random.randint(jax.random.fold_in(key, 502), (TOKENS,), 0, 16)
    inside = jnp.arange(TOKENS) % TOK_DEV != 0
    raw_rows = (coin == 0) & inside & jnp.logical_not(starts)
    after_rows = jnp.concatenate([raw_rows[1:], jnp.zeros((1,), jnp.bool_)])
    return raw_rows & jnp.logical_not(after_rows)


def shaped_keys(key):
    key_base = jax.random.truncated_normal(jax.random.fold_in(key, 503), -4.0, 4.0, (TOKENS, KVD), jnp.float32)
    chosen = pick_rows(key)
    before_chosen = jnp.concatenate([chosen[1:], jnp.zeros((1,), jnp.bool_)])
    mixed = key_base
    return jnp.where(before_chosen[:, None], mixed, key_base)


def draw_doc_ids(key, part):
    starts = mark_starts(key)
    counted = (jnp.cumsum(starts.astype(jnp.int32)) - 1).astype(jnp.int32)
    last_token = jnp.arange(TOKENS) == TOKENS - 1
    return jnp.where(last_token, TOKENS - 1, counted).astype(jnp.int32)


def draw_keys(key, part):
    return shaped_keys(key).astype(jnp.bfloat16)


def draw_queries(key, part):
    key_own = jax.random.fold_in(key, 8)
    drawn = jax.random.truncated_normal(key_own, -4.0, 4.0, (TOKENS, QD), jnp.float32)
    return drawn.astype(jnp.bfloat16)


def draw_inputs(key, part):
    key_own = jax.random.fold_in(key, 9)
    drawn = jax.random.truncated_normal(key_own, -4.0, 4.0, (TOKENS, D), jnp.float32)
    return drawn.astype(jnp.bfloat16)


def level_of(rng, shape, shards, smallest, largest):
    loudness, own = 1.0, jax.random.fold_in(rng, 6)
    for axis_at, parts in shards:
        heights = jnp.exp(jax.random.uniform(jax.random.fold_in(own, axis_at), (parts,), jnp.float32, smallest / len(shards), largest / len(shards)))
        loudness = loudness * jnp.repeat(heights, shape[axis_at] // parts).reshape([-1 if axis == axis_at else 1 for axis in range(len(shape))])
    return loudness


def noise(key, dims, scale, reach, shards=(), kind=jnp.bfloat16):
    array = jax.random.normal(key, dims, jnp.float32) * scale
    if len(shards) > 0:
        array = level_of(key, dims, shards, -0.22, 0.18) * array
    return jnp.clip(array, min=-reach, max=reach).astype(kind)


def setup_inputs(seed: int = 0) -> dict:
    arg_keys = jax.random.split(jax.random.key(seed), 9)
    return {
        "inputs": draw_inputs(jax.random.fold_in(arg_keys[8], 71), 0),
        "queries": draw_queries(jax.random.fold_in(arg_keys[8], 71), 0),
        "keys": draw_keys(jax.random.fold_in(arg_keys[8], 71), 0),
        "doc_ids": draw_doc_ids(jax.random.fold_in(arg_keys[8], 71), 0),
        "grad_out": noise(arg_keys[4], (TOKENS, QD), 1.0, 6.0, ((0, 512),)),
        "gain": jnp.clip(1.0 + 0.15 * jax.random.normal(arg_keys[5], (D,), jnp.float32), 0.25, 1.75),
        "bias": noise(arg_keys[6], (KVD,), 0.5, 3.0, (), jnp.float32),
        "w_value": noise(arg_keys[7], (D, KVD), D ** -0.5, 0.078125, ((0, 16),)),
    }


def norm_forward(inputs, gain):
    values = inputs.astype(jnp.float32)
    inverse_rms = lax.rsqrt(lax.optimization_barrier(jnp.mean(values * values, axis=-1, keepdims=True)) + 1e-06)
    normed = values * inverse_rms
    return (normed, inverse_rms, (normed * gain).astype(jnp.bfloat16))

def attend(queries, keys, doc_ids, value_rows, grad_rows):
    row_count = queries.shape[0]
    kv_heads = keys.shape[1] // HD
    group_size = queries.shape[1] // keys.shape[1]
    query_heads = queries.astype(jnp.float32).reshape(row_count, kv_heads, group_size, HD)
    key_heads = keys.astype(jnp.float32).reshape(row_count, kv_heads, HD)
    scores = jnp.einsum('qgjd,kgd->gjqk', query_heads, key_heads) * (1.0 / math.sqrt(HD))
    positions = jnp.arange(row_count)
    allowed = (positions[:, None] >= positions[None, :]) & (doc_ids[:, None] == doc_ids[None, :])
    scores = jnp.where(allowed, scores, -1e+30)
    row_max = lax.optimization_barrier(jnp.max(scores, axis=-1, keepdims=True))
    exponent = jnp.exp(scores - row_max)
    probabilities = (exponent / lax.optimization_barrier(jnp.sum(exponent, axis=-1, keepdims=True))).astype(jnp.bfloat16)
    prob_wide = probabilities.astype(jnp.float32)
    value_heads = value_rows.astype(jnp.float32).reshape(row_count, kv_heads, HD)
    attention = jnp.einsum('gjqk,kgd->qgjd', prob_wide, value_heads).reshape(row_count, queries.shape[1]).astype(jnp.bfloat16)
    grad_heads = grad_rows.astype(jnp.float32).reshape(row_count, kv_heads, group_size, HD)
    value_grad = jnp.einsum('gjqk,qgjd->kgd', prob_wide, grad_heads).reshape(row_count, keys.shape[1])
    return (attention, value_grad)

def reference(inputs, queries, keys, doc_ids, grad_out, gain, bias, w_value):
    slab_count = TOKENS // TOK_DEV
    stacked = (inputs.reshape(slab_count, TOK_DEV, D), queries.reshape(slab_count, TOK_DEV, QD), keys.reshape(slab_count, TOK_DEV, KVD), doc_ids.reshape(slab_count, TOK_DEV), grad_out.reshape(slab_count, TOK_DEV, QD))

    def one_slab(carried, slab_rows):
        weight_sum, gain_sum, bias_sum = carried
        slab_inputs, slab_queries, slab_keys, slab_docs, slab_grads = slab_rows
        normed, inverse_rms, hidden = norm_forward(slab_inputs, gain)
        value = (jnp.dot(hidden, w_value, preferred_element_type=jnp.float32) + bias).astype(jnp.bfloat16)
        attention, value_grad = attend(slab_queries, slab_keys, slab_docs, value, slab_grads)
        value_grad_b = value_grad.astype(jnp.bfloat16)
        weight_term = jnp.dot(hidden.T, value_grad_b, preferred_element_type=jnp.float32)
        hidden_grad = jnp.dot(value_grad_b, w_value.T, preferred_element_type=jnp.float32).astype(jnp.bfloat16)
        hidden_wide = hidden_grad.astype(jnp.float32)
        gain_term = lax.optimization_barrier(jnp.sum(hidden_wide * normed, axis=0))
        normed_grad = hidden_wide * gain
        grad_inputs = (inverse_rms * (normed_grad - normed * lax.optimization_barrier(jnp.mean(normed_grad * normed, axis=-1, keepdims=True)))).astype(jnp.bfloat16)
        new_carry = (weight_sum + weight_term, gain_sum + gain_term, bias_sum + lax.optimization_barrier(jnp.sum(value_grad, axis=0)))
        return (new_carry, (attention, grad_inputs))
    start_carry = (jnp.zeros((D, KVD), jnp.float32), jnp.zeros((D,), jnp.float32), jnp.zeros((KVD,), jnp.float32))
    totals, slab_outs = lax.scan(one_slab, start_carry, stacked)
    attention = slab_outs[0].reshape(TOKENS, QD)
    grad_inputs = slab_outs[1].reshape(TOKENS, D)
    return (attention, grad_inputs, totals[0] / N_DP, totals[1] / N_DP, totals[2] / N_DP)
```

```python
import math

import jax
import jax.numpy as jnp
from jax import lax
from jax.experimental import pallas as pl
from jax.experimental.pallas import tpu as pltpu
from jax.sharding import PartitionSpec as P

MESH = pl.DeviceIdType.MESH
F32, BF16 = jnp.float32, jnp.bfloat16

D = 5120
HD = 128
ROWS = 128
GROUPS = 4
PER_GROUP = 5
KV = GROUPS * HD
QD = KV * PER_GROUP
NX, NY, NZ = 4, 4, 16
SHARE = 320
PAIR = 2 * SHARE
BLOCKS = D // PAIR
WIDE = 384
COLUMNS = 16
SMALL = PAIR + KV
N_DP = 32
COPIES = 95


def dot(a, b, dims):
    return lax.dot_general(a, b, (dims, ((), ())), preferred_element_type=F32)


def lane_tiles(a):
    total = a[:, :HD]
    for i in range(1, a.shape[1] // HD):
        total = total + a[:, i * HD : (i + 1) * HD]
    return total


def kernel(
    x_any, q_any, k_any, go_any, doc_ref, gain_ref, bias_ref, w_any,
    att_any, gi_any, gw_ref, gg_ref, gb_ref,
    xv, qv, kv, gov, hid, inv_ref, prob, vgb, vt, wf, xh, bias_term, value,
    hgrad, att, gi, pt, yr, zs, zr, small, sx, sy_own, sy, sz_own, sz, sg_own, sg,
    local_sem, send_sem, recv_sem,
):
    blk, dp = lax.axis_index("blk"), lax.axis_index("dp")
    x, yh, c = lax.div(blk, 4), lax.rem(lax.div(blk, 2), 2), lax.rem(blk, 2)
    z, yl = lax.div(dp, 2), lax.rem(dp, 2)
    y, half = yh * 2 + yl, lax.rem(z, 2)
    me = x * 2 + c

    def place(x, yh, c, z, yl):
        return (x * 4 + yh * 2 + c, z * 2 + yl)

    def on_y(y, c):
        return place(x, lax.div(y, 2), c, z, lax.rem(y, 2))

    def plus(a, by, n):
        return lax.rem(a + by, n)

    used = [0]

    def remote(src, dst, to):
        i = used[0]
        used[0] += 1
        return pltpu.make_async_remote_copy(
            src_ref=src,
            dst_ref=dst,
            send_sem=send_sem.at[i],
            recv_sem=recv_sem.at[i],
            device_id=to,
            device_id_type=MESH,
        )

    sent = []

    def send(src, dst, to):
        copy = remote(src, dst, to)
        copy.start()
        sent.append(copy)
        return copy

    loads = [
        pltpu.make_async_copy(w_any.at[pl.ds(0, 160)], wf.at[x, yh, c, 0], local_sem.at[0]),
        pltpu.make_async_copy(w_any.at[pl.ds(160, 160)], wf.at[x, yh, c, 1], local_sem.at[1]),
        pltpu.make_async_copy(x_any, xv, local_sem.at[2]),
        pltpu.make_async_copy(q_any, qv, local_sem.at[3]),
        pltpu.make_async_copy(k_any, kv, local_sem.at[4]),
        pltpu.make_async_copy(go_any, gov, local_sem.at[5]),
    ]
    for copy in loads:
        copy.start()

    near = [(dx, dc) for dx in (2, 1, 3, 0) for dc in (0, 1) if (dx, dc) != (0, 0)]
    sibling = place(x, yh, 1 - c, z, yl)
    across = place(x, 1 - yh, c, z, 1 - yl)

    barrier = pltpu.get_barrier_semaphore()
    partners = [place(plus(x, dx, NX), yh, plus(c, dc, 2), z, yl) for dx, dc in near]
    partners += [on_y(plus(y, dy, NY), plus(c, dc, 2)) for dy in (1, 2, 3) for dc in (0, 1)]
    partners += [place(x, yh, c, plus(z, dz, NZ), yl) for dz in range(1, NZ)]
    for partner in partners:
        pl.semaphore_signal(barrier, inc=1, device_id=partner, device_id_type=MESH)
    pl.semaphore_wait(barrier, len(partners))

    def block(k, y_hi, h):
        return wf.at[plus(x, NX - k, NX), y_hi, c, h]

    def pass_on(ref, to):
        return send(ref, ref, to)

    loads[0].wait()
    loads[1].wait()
    along_x, along_y, along_z, beside = {}, {}, {}, []
    for k in (2, 1, 3):
        along_x[k] = pass_on(block(0, yh, half), place(plus(x, k, NX), yh, c, z, yl))
    along_y[0] = pass_on(block(0, yh, half), across)
    beside.append(pass_on(block(0, yh, half), sibling))
    beside.append(pass_on(block(0, yh, 1 - half), sibling))

    loads[2].wait()

    def squares(j, total):
        part = xv[:, pl.ds(pl.multiple_of(j * PAIR, HD), PAIR)].astype(F32)
        return total + lane_tiles(part * part)

    total = lax.fori_loop(0, BLOCKS, squares, jnp.zeros((ROWS, HD), F32))
    inverse = lax.rsqrt(jnp.sum(total, axis=1, keepdims=True) * (1.0 / D) + 1e-06)
    inv_ref[...] = jnp.broadcast_to(inverse, (ROWS, HD))

    def normalise(j, carry):
        columns = pl.ds(pl.multiple_of(j * PAIR, HD), PAIR)
        normed = xv[:, columns].astype(F32) * inv_ref[:, :1]
        hid[j] = (normed * gain_ref[:, columns]).astype(BF16)
        return carry

    lax.fori_loop(0, BLOCKS, normalise, 0)

    hidden_sent = []
    for dx, dc in near:
        to_x, to_c = plus(x, dx, NX), plus(c, dc, 2)
        hidden_sent.append(send(hid.at[to_x * 2 + to_c], xh.at[me], place(to_x, yh, to_c, z, yl)))
    xh[me] = hid[me]

    up = place(x, yh, c, plus(z, 1, NZ), yl)
    down = place(x, yh, c, plus(z, NZ - 1, NZ), yl)

    def spread(k, y_hi, is_up, key):
        along_z[key] = pass_on(block(k, y_hi, half), up if is_up else down)
        beside.append(pass_on(block(k, y_hi, half), sibling))

    for k in (1, 3, 2):
        along_x[k].wait_recv()
        along_y[k] = pass_on(block(k, yh, half), across)
        spread(k, yh, k != 3, (0, k))

    for copy in loads[3:]:
        copy.wait()
    doc_row = jnp.broadcast_to(doc_ref[...].astype(F32), (ROWS, ROWS))
    positions = lax.broadcasted_iota(jnp.int32, (ROWS, ROWS), 0)
    key_positions = lax.broadcasted_iota(jnp.int32, (ROWS, ROWS), 1)
    allowed = (positions >= key_positions) & (doc_row == doc_row.T)

    def stacked(ref, g):
        heads = range(g * PER_GROUP, (g + 1) * PER_GROUP)
        return jnp.concatenate([ref[:, h * HD : (h + 1) * HD] for h in heads], axis=0)

    for g in range(GROUPS):
        group = slice(g * HD, (g + 1) * HD)
        scores = dot(stacked(qv, g), kv[:, group], ((1,), (1,))) * (1.0 / math.sqrt(HD))
        scores = jnp.where(allowed[None], scores.reshape(PER_GROUP, ROWS, ROWS), -1e30)
        exponent = jnp.exp(scores - jnp.max(scores, axis=-1, keepdims=True))
        chances = exponent / jnp.sum(exponent, axis=-1, keepdims=True)
        chances = chances.reshape(PER_GROUP * ROWS, ROWS).astype(BF16)
        prob[g] = chances
        value_grad = dot(chances, stacked(gov, g), ((0,), (0,)))
        bias_term[:, group] = jnp.sum(value_grad, axis=0, keepdims=True)
        vgb[:, group] = value_grad.astype(BF16)
        vt[group, pl.ds(pl.multiple_of(me * HD, HD), HD)] = value_grad.T.astype(BF16)

    def turned(x, c):
        return vt.at[:, pl.ds(pl.multiple_of((x * 2 + c) * HD, HD), HD)]

    turned_x = {}
    for k in (2, 1, 3):
        turned_x[k] = pass_on(turned(x, c), place(plus(x, k, NX), yh, c, z, yl))
    turned_beside = [pass_on(turned(x, c), sibling)]

    for k in (0, 1, 3, 2):
        along_y[k].wait_recv()
        spread(k, 1 - yh, k in (0, 3), (1, k))
    for k in (1, 3, 2):
        turned_x[k].wait_recv()
        turned_beside.append(pass_on(turned(plus(x, NX - k, NX), c), sibling))
    for (other, k), copy in along_z.items():
        copy.wait_recv()
        beside.append(pass_on(block(k, 1 - yh if other else yh, 1 - half), sibling))

    for copy in hidden_sent + turned_beside:
        copy.wait_recv()

    def product(i, carry):
        rows = pl.ds(pl.multiple_of(i * 128, 128), 128)
        part = dot(vt[rows, :], xh[...].reshape(8 * ROWS, PAIR), ((1,), (0,)))
        part = part.astype(BF16).reshape(4, 2, COLUMNS, PAIR)
        to = pl.ds(pl.multiple_of(i * 64, 64), 64)
        pt[0, to, :] = part[:, 0].reshape(64, PAIR)
        pt[1, to, :] = part[:, 1].reshape(64, PAIR)
        return carry

    lax.fori_loop(0, 4, product, 0)

    y_first = used[0]
    used[0] += 4
    crossing = []
    for side in (0, 1):
        for to_c in (0, 1):
            i = y_first + side * 2 + to_c
            to_y = 2 * c + side
            src, dst = pt.at[side, :, pl.ds(to_c * 256, WIDE)], yr.at[y]
            mine = (to_y == y) & (c == to_c)
            there = pltpu.make_async_remote_copy(
                src_ref=src,
                dst_ref=dst,
                send_sem=send_sem.at[i],
                recv_sem=recv_sem.at[y_first + y],
                device_id=on_y(to_y, to_c),
                device_id_type=MESH,
            )
            here = pltpu.make_async_copy(src, dst, recv_sem.at[y_first + y])
            crossing.append((mine, there))

            @pl.when(mine)
            def _():
                here.start()

            @pl.when(jnp.logical_not(mine))
            def _():
                there.start()

    for copy in beside:
        copy.wait_recv()

    value[...] = jnp.zeros_like(value)

    def with_block(j, row_sum):
        columns = pl.ds(pl.multiple_of(j * PAIR, HD), PAIR)
        weights = wf[lax.div(j, 2), lax.rem(j, 2)].reshape(PAIR, KV)
        value[...] += dot(hid[j], weights, ((1,), (0,)))
        back = dot(vgb[...], weights, ((1,), (1,))).astype(BF16)
        hgrad[j] = back
        wide = back.astype(F32) * (xv[:, columns].astype(F32) * inv_ref[:, :1])
        small[j, :, :PAIR] = jnp.sum(wide, axis=0, keepdims=True)
        small[j, :, PAIR:] = bias_term[...]
        return row_sum + lane_tiles(wide * gain_ref[:, columns])

    row_sum = lax.fori_loop(0, BLOCKS, with_block, jnp.zeros((ROWS, HD), F32))

    small_sent = []
    for dx, dc in near:
        to_x, to_c = plus(x, dx, NX), plus(c, dc, 2)
        small_sent.append(send(small.at[to_x * 2 + to_c], sx.at[me], place(to_x, yh, to_c, z, yl)))
    sx[me] = small[me]

    value_b = (value[...] + bias_ref[...]).astype(BF16)
    for g in range(GROUPS):
        mixed = dot(prob[g], value_b[:, g * HD : (g + 1) * HD], ((1,), (0,))).astype(BF16)
        for i in range(PER_GROUP):
            h = g * PER_GROUP + i
            att[:, h * HD : (h + 1) * HD] = mixed[i * ROWS : (i + 1) * ROWS]
    att_out = pltpu.make_async_copy(att, att_any, local_sem.at[6])
    att_out.start()

    for copy in small_sent:
        copy.wait_recv()
    sy_own[...] = jnp.sum(sx[...], axis=0)
    small_y = [send(sy_own, sy.at[y], on_y(plus(y, dy, NY), c)) for dy in (1, 2, 3)]
    sy[y] = sy_own[...]

    for i in range(NY):
        pltpu.make_async_copy(yr.at[i], yr.at[i], recv_sem.at[y_first + i]).wait()
    over_y = yr[0].astype(F32)
    for i in range(1, NY):
        over_y = over_y + yr[i].astype(F32)
    zs[...] = over_y.astype(BF16).reshape(NZ, COLUMNS, WIDE)
    columns_z = []
    for dz in range(1, NZ):
        to_z = plus(z, dz, NZ)
        columns_z.append(send(zs.at[to_z], zr.at[z], place(x, yh, c, to_z, yl)))
    zr[z] = zs[z]

    for copy in small_y:
        copy.wait_recv()
    sz_own[...] = jnp.sum(sy[...], axis=0)
    small_z = []
    for dz in range(1, NZ):
        small_z.append(send(sz_own, sz.at[z], place(x, yh, c, plus(z, dz, NZ), yl)))
    sz[z] = sz_own[...]

    mean = jnp.sum(row_sum, axis=1, keepdims=True) * (1.0 / D)

    def inputs_gradient(j, carry):
        columns = pl.ds(pl.multiple_of(j * PAIR, HD), PAIR)
        inverse = inv_ref[:, :1]
        normed = xv[:, columns].astype(F32) * inverse
        scaled = hgrad[j].astype(F32) * gain_ref[:, columns]
        gi[:, columns] = (inverse * (scaled - normed * mean)).astype(BF16)
        return carry

    lax.fori_loop(0, BLOCKS, inputs_gradient, 0)
    gi_out = pltpu.make_async_copy(gi, gi_any, local_sem.at[7])
    gi_out.start()

    for copy in small_z:
        copy.wait_recv()
    small_total = jnp.sum(sz[...], axis=0) * (1.0 / N_DP)
    sg_own[...] = small_total[:, :PAIR]
    gb_ref[...] = small_total[:, PAIR:]
    gathered = []
    for dx, dc in near:
        to = place(plus(x, dx, NX), yh, plus(c, dc, 2), z, yl)
        gathered.append(send(sg_own, sg.at[me], to))
    sg[me] = sg_own[...]

    for copy in columns_z:
        copy.wait_recv()
    over_z = zr[0].astype(F32)
    for i in range(1, NZ):
        over_z = over_z + zr[i].astype(F32)
    over_z = over_z * (1.0 / N_DP)
    gw_ref[...] = jnp.where(c == 0, over_z[:, :SHARE], over_z[:, WIDE - SHARE :])

    for copy in gathered:
        copy.wait_recv()
    gg_ref[...] = sg[...]

    for copy in sent:
        copy.wait_send()
    for mine, there in crossing:

        @pl.when(jnp.logical_not(mine))
        def _():
            there.wait_send()

    att_out.wait()
    gi_out.wait()


def local(inputs, queries, keys, doc_ids, grad_out, gain, bias, w_value):
    whole = pl.BlockSpec(memory_space=pltpu.VMEM)
    anywhere = pl.BlockSpec(memory_space=pl.ANY)
    attention, grad_inputs, grad_w, grad_gain, grad_bias = pl.pallas_call(
        kernel,
        out_shape=(
            jax.ShapeDtypeStruct((ROWS, QD), BF16),
            jax.ShapeDtypeStruct((ROWS, D), BF16),
            jax.ShapeDtypeStruct((COLUMNS, SHARE), F32),
            jax.ShapeDtypeStruct((BLOCKS, 1, PAIR), F32),
            jax.ShapeDtypeStruct((1, KV), F32),
        ),
        in_specs=[anywhere] * 4 + [whole] * 3 + [anywhere],
        out_specs=(anywhere, anywhere, whole, whole, whole),
        scratch_shapes=[
            pltpu.VMEM((ROWS, D), BF16),
            pltpu.VMEM((ROWS, QD), BF16),
            pltpu.VMEM((ROWS, KV), BF16),
            pltpu.VMEM((ROWS, QD), BF16),
            pltpu.VMEM((BLOCKS, ROWS, PAIR), BF16),
            pltpu.VMEM((ROWS, HD), F32),
            pltpu.VMEM((GROUPS, PER_GROUP * ROWS, ROWS), BF16),
            pltpu.VMEM((ROWS, KV), BF16),
            pltpu.VMEM((KV, 8 * ROWS), BF16),
            pltpu.VMEM((NX, 2, 2, 2, SHARE // 2, KV), BF16),
            pltpu.VMEM((8, ROWS, PAIR), BF16),
            pltpu.VMEM((1, KV), F32),
            pltpu.VMEM((ROWS, KV), F32),
            pltpu.VMEM((BLOCKS, ROWS, PAIR), BF16),
            pltpu.VMEM((ROWS, QD), BF16),
            pltpu.VMEM((ROWS, D), BF16),
            pltpu.VMEM((2, KV // 2, PAIR), BF16),
            pltpu.VMEM((NY, KV // 2, WIDE), BF16),
            pltpu.VMEM((NZ, COLUMNS, WIDE), BF16),
            pltpu.VMEM((NZ, COLUMNS, WIDE), BF16),
            pltpu.VMEM((BLOCKS, 1, SMALL), F32),
            pltpu.VMEM((8, 1, SMALL), F32),
            pltpu.VMEM((1, SMALL), F32),
            pltpu.VMEM((NY, 1, SMALL), F32),
            pltpu.VMEM((1, SMALL), F32),
            pltpu.VMEM((NZ, 1, SMALL), F32),
            pltpu.VMEM((1, PAIR), F32),
            pltpu.VMEM((8, 1, PAIR), F32),
            pltpu.SemaphoreType.DMA((8,)),
            pltpu.SemaphoreType.DMA((COPIES,)),
            pltpu.SemaphoreType.DMA((COPIES,)),
        ],
        compiler_params=pltpu.CompilerParams(
            collective_id=0, has_side_effects=True, vmem_limit_bytes=40 * 1024 * 1024
        ),
    )(
        inputs, queries, keys, grad_out, doc_ids.reshape(1, ROWS), gain.reshape(1, D),
        bias.reshape(1, KV), w_value,
    )
    return attention, grad_inputs, grad_w.T, grad_gain.reshape(D), grad_bias.reshape(KV)


def solution(mesh):
    placed = (
        P(("blk", "dp"), None),
        P(("blk", "dp"), None),
        P(("blk", "dp"), None),
        P(("blk", "dp")),
        P(("blk", "dp"), None),
        P(),
        P(),
        P("blk", None),
    )
    return jax.shard_map(
        local,
        mesh=mesh,
        in_specs=placed,
        out_specs=(P(("blk", "dp"), None), P(("blk", "dp"), None), P("blk", "dp"), P(), P()),
        check_vma=False,
    )
```

```python
import math

import jax
import jax.numpy as jnp
from jax import lax
from jax.experimental import pallas as pl
from jax.experimental.pallas import tpu as pltpu
from jax.sharding import PartitionSpec as P

MESH = pl.DeviceIdType.MESH
F32, BF16 = jnp.float32, jnp.bfloat16

D = 5120
HD = 128
ROWS = 128
GROUPS = 4
PER_GROUP = 5
KV = GROUPS * HD
QD = KV * PER_GROUP
NX, NY, NZ = 4, 4, 16
SHARE = 320
QUARTER = SHARE // 4
PAIR = 2 * SHARE
BLOCKS = D // PAIR
WIDE = 384
COLUMNS = 16
SMALL = PAIR + KV
N_DP = 32
COPIES = 120
PIECES = 4


def dot(a, b, dims):
    return lax.dot_general(a, b, (dims, ((), ())), preferred_element_type=F32)


def lane_tiles(a):
    total = a[:, :HD]
    for i in range(1, a.shape[1] // HD):
        total = total + a[:, i * HD : (i + 1) * HD]
    return total


def kernel(
    x_any, q_any, k_any, go_any, doc_ref, gain_ref, bias_ref, w_any,
    att_any, gi_any, gw_ref, gg_ref, gb_ref,
    xv, qv, kv, gov, hid, inv_ref, prob, vgb, vt, wf, xh, value,
    hgrad, att, gi, pt, yr, zs, zr, sy_own, sy, sz_own, sz, sg_own, sg,
    local_sem, send_sem, recv_sem, lower_sem, upper_sem,
):
    blk, dp = lax.axis_index("blk"), lax.axis_index("dp")
    x, yh, c = lax.div(blk, 4), lax.rem(lax.div(blk, 2), 2), lax.rem(blk, 2)
    z, yl = lax.div(dp, 2), lax.rem(dp, 2)
    y, half = yh * 2 + yl, lax.rem(z, 2)
    me = x * 2 + c

    def place(x, yh, c, z, yl):
        return (x * 4 + yh * 2 + c, z * 2 + yl)

    def on_y(y, c):
        return place(x, lax.div(y, 2), c, z, lax.rem(y, 2))

    def plus(a, by, n):
        return lax.rem(a + by, n)

    used = [0]

    def take(n):
        used[0] += n
        return used[0] - n

    def remote(src, dst, to, sent_at, received_at):
        return pltpu.make_async_remote_copy(
            src_ref=src,
            dst_ref=dst,
            send_sem=send_sem.at[sent_at],
            recv_sem=recv_sem.at[received_at],
            device_id=to,
            device_id_type=MESH,
        )

    sent = []

    def send(src, dst, to):
        i = take(1)
        copy = remote(src, dst, to, i, i)
        copy.start()
        sent.append(copy)
        return copy

    def pass_on(ref, to):
        return send(ref, ref, to)

    loads = [
        pltpu.make_async_copy(x_any, xv, local_sem.at[0]),
        pltpu.make_async_copy(q_any, qv, local_sem.at[1]),
        pltpu.make_async_copy(k_any, kv, local_sem.at[2]),
        pltpu.make_async_copy(go_any, gov, local_sem.at[3]),
    ]
    loads += [
        pltpu.make_async_copy(
            w_any.at[pl.ds(i * QUARTER, QUARTER)], wf.at[x, yh, c, i], local_sem.at[4 + i]
        )
        for i in range(4)
    ]
    for copy in loads:
        copy.start()

    near = [(dx, dc) for dx in (2, 1, 3, 0) for dc in (0, 1) if (dx, dc) != (0, 0)]
    sibling = place(x, yh, 1 - c, z, yl)
    up = place(x, yh, c, plus(z, 1, NZ), yl)
    down = place(x, yh, c, plus(z, NZ - 1, NZ), yl)

    barrier = pltpu.get_barrier_semaphore()
    partners = [place(plus(x, dx, NX), yh, plus(c, dc, 2), z, yl) for dx, dc in near]
    partners += [on_y(plus(y, dy, NY), plus(c, dc, 2)) for dy in (1, 2, 3) for dc in (0, 1)]
    partners += [up, down]
    for partner in partners:
        pl.semaphore_signal(barrier, inc=1, device_id=partner, device_id_type=MESH)

    loads[0].wait()

    def squares(j, total):
        part = xv[:, pl.ds(pl.multiple_of(j * PAIR, HD), PAIR)].astype(F32)
        return total + lane_tiles(part * part)

    total = lax.fori_loop(0, BLOCKS, squares, jnp.zeros((ROWS, HD), F32))
    inverse = lax.rsqrt(jnp.sum(total, axis=1, keepdims=True) * (1.0 / D) + 1e-06)
    inv_ref[...] = jnp.broadcast_to(inverse, (ROWS, HD))

    pl.semaphore_wait(barrier, len(partners))

    rounds = [0]

    def relay():
        if rounds[0] > 0:
            pl.semaphore_wait(lower_sem, 1)
            pl.semaphore_wait(upper_sem, 1)
        if rounds[0] < NZ // 2 - 1:
            pl.semaphore_signal(lower_sem, inc=1, device_id=up, device_id_type=MESH)
            pl.semaphore_signal(upper_sem, inc=1, device_id=down, device_id_type=MESH)
        rounds[0] += 1

    relay()

    def quarter(k, y_hi, y_lo):
        return wf.at[plus(x, NX - k, NX), y_hi, c, half * 2 + y_lo]

    def half_block(k, y_hi, h):
        return wf.at[plus(x, NX - k, NX), y_hi, c, pl.ds(h * 2, 2)]

    for copy in loads[4:]:
        copy.wait()
    along_x, along_y, along_z, beside = {}, {}, {}, {}

    others = (
        place(x, yh, c, z, 1 - yl),
        place(x, 1 - yh, c, z, yl),
        place(x, 1 - yh, c, z, 1 - yl),
    )

    def spread_y(k):
        for i in range(1 if k == 0 else 0, 3):
            along_y[k, i] = pass_on(quarter(k, yh, yl), others[i])

    def spread_z(k, other, is_up):
        y_hi = 1 - yh if other else yh
        along_z[other, k] = pass_on(half_block(k, y_hi, half), up if is_up else down)
        beside[other, k, 0] = pass_on(half_block(k, y_hi, half), sibling)

    def spread_beside(k, other):
        along_z[other, k].wait_recv()
        y_hi = 1 - yh if other else yh
        beside[other, k, 1] = pass_on(half_block(k, y_hi, 1 - half), sibling)

    spread_y(0)
    beside[0, 0, 0] = pass_on(half_block(0, yh, 0), sibling)
    beside[0, 0, 1] = pass_on(half_block(0, yh, 1), sibling)
    for k in (2, 1, 3):
        along_x[k] = pass_on(quarter(0, yh, yl), place(plus(x, k, NX), yh, c, z, yl))

    def normalise(j, carry):
        columns = pl.ds(pl.multiple_of(j * PAIR, HD), PAIR)
        normed = xv[:, columns].astype(F32) * inv_ref[:, :1]
        hid[j] = (normed * gain_ref[:, columns]).astype(BF16)
        return carry

    lax.fori_loop(0, BLOCKS, normalise, 0)

    def send_hidden(first, width):
        columns = pl.ds(first, width)
        copies = []
        for dx, dc in near:
            to_x, to_c = plus(x, dx, NX), plus(c, dc, 2)
            src, dst = hid.at[to_x * 2 + to_c, :, columns], xh.at[me, :, columns]
            copies.append(send(src, dst, place(to_x, yh, to_c, z, yl)))
        return copies

    hidden_a = send_hidden(0, WIDE)
    xh[me] = hid[me]

    for copy in loads[1:4]:
        copy.wait()
    doc_row = jnp.broadcast_to(doc_ref[...].astype(F32), (ROWS, ROWS))
    positions = lax.broadcasted_iota(jnp.int32, (ROWS, ROWS), 0)
    key_positions = lax.broadcasted_iota(jnp.int32, (ROWS, ROWS), 1)
    allowed = (positions >= key_positions) & (doc_row == doc_row.T)

    def stacked(ref, g):
        heads = range(g * PER_GROUP, (g + 1) * PER_GROUP)
        return jnp.concatenate([ref[:, h * HD : (h + 1) * HD] for h in heads], axis=0)

    for g in range(GROUPS):
        group = slice(g * HD, (g + 1) * HD)
        scores = dot(stacked(qv, g), kv[:, group], ((1,), (1,))) * (1.0 / math.sqrt(HD))
        scores = jnp.where(allowed[None], scores.reshape(PER_GROUP, ROWS, ROWS), -1e30)
        exponent = jnp.exp(scores - jnp.max(scores, axis=-1, keepdims=True))
        chances = exponent / jnp.sum(exponent, axis=-1, keepdims=True)
        chances = chances.reshape(PER_GROUP * ROWS, ROWS).astype(BF16)
        prob[g] = chances
        value_grad = dot(chances, stacked(gov, g), ((0,), (0,)))
        vgb[:, group] = value_grad.astype(BF16)
        vt[group, pl.ds(pl.multiple_of(me * HD, HD), HD)] = value_grad.T.astype(BF16)

    def turned(x, c):
        return vt.at[:, pl.ds(pl.multiple_of((x * 2 + c) * HD, HD), HD)]

    turned_x = {}
    for k in (2, 1, 3):
        turned_x[k] = pass_on(turned(x, c), place(plus(x, k, NX), yh, c, z, yl))
    turned_beside = [pass_on(turned(x, c), sibling)]
    hidden_b = send_hidden(WIDE, PAIR - WIDE)
    relay()

    for i in (1, 2):
        along_y[0, i].wait_recv()
    spread_z(0, 1, True)
    relay()
    for k in (1, 3, 2):
        along_x[k].wait_recv()
        spread_y(k)
    relay()
    spread_beside(0, 1)
    relay()
    for k in (1, 3, 2):
        for i in range(3):
            along_y[k, i].wait_recv()
        spread_z(k, 0, k != 3)
        spread_z(k, 1, k == 3)
    relay()

    for k in (1, 3, 2):
        turned_x[k].wait_recv()
        turned_beside.append(pass_on(turned(plus(x, NX - k, NX), c), sibling))
    relay()

    def product(first, width):
        def step(i, carry):
            rows = pl.ds(pl.multiple_of(i * 128, 128), 128)
            columns = slice(first, first + width)
            part = dot(vt[rows, :], xh[:, :, columns].reshape(8 * ROWS, width), ((1,), (0,)))
            part = part.astype(BF16).reshape(4, 2, COLUMNS, width)
            to = pl.ds(pl.multiple_of(i * 64, 64), 64)
            pt[0, to, columns] = part[:, 0].reshape(64, width)
            pt[1, to, columns] = part[:, 1].reshape(64, width)
            return carry

        lax.fori_loop(0, 4, step, 0)

    y_sent, y_received = take(4), used[0] - 4
    crossing = []

    def send_y(to_c):
        for side in (0, 1):
            to_y = 2 * c + side
            src, dst = pt.at[side, :, pl.ds(to_c * 256, WIDE)], yr.at[y]
            mine = (to_y == y) & (c == to_c)
            there = remote(src, dst, on_y(to_y, to_c), y_sent + side * 2 + to_c, y_received + y)
            here = pltpu.make_async_copy(src, dst, recv_sem.at[y_received + y])
            crossing.append((mine, there))

            @pl.when(mine)
            def _():
                here.start()

            @pl.when(jnp.logical_not(mine))
            def _():
                there.start()

    z_first = take(NZ - 1)
    columns_z = []
    for dz in range(1, NZ):
        to_z = plus(z, dz, NZ)
        i = z_first + dz - 1
        columns_z.append(remote(zs.at[to_z], zr.at[z], place(x, yh, c, to_z, yl), i, i))

    def sum_y():
        for i in range(NY):
            pltpu.make_async_copy(yr.at[i], yr.at[i], recv_sem.at[y_received + i]).wait()
        over_y = yr[0].astype(F32)
        for i in range(1, NY):
            over_y = over_y + yr[i].astype(F32)
        zs[...] = over_y.astype(BF16).reshape(NZ, COLUMNS, WIDE)
        for copy in columns_z:
            copy.start()
        zr[z] = zs[z]

    for copy in hidden_a + turned_beside:
        copy.wait_recv()
    product(0, WIDE)
    send_y(0)
    relay()
    pl.when(c == 0)(sum_y)

    for copy in hidden_b:
        copy.wait_recv()
    product(WIDE, PAIR - WIDE)
    send_y(1)

    for key in ((0, 0, 0), (0, 0, 1), (1, 0, 0), (1, 0, 1)):
        beside.pop(key).wait_recv()
    ones = jnp.ones((8, 8 * ROWS), BF16)
    sy_own[:, PAIR:] = dot(ones, vt[...], ((1,), (1,)))[:1]

    def weighted(i, total):
        columns = pl.ds(pl.multiple_of(i * 128, 128), 128)
        turned_w = wf[x, c, :, :, :, columns].reshape(PAIR, 128).astype(F32).T
        turned_w = turned_w.reshape(4, 2, COLUMNS, PAIR)
        rows = pl.ds(pl.multiple_of(i * 64, 64), 64)
        for side in (0, 1):
            both = pt[side, rows, :].astype(F32) * turned_w[:, side].reshape(64, PAIR)
            total = total + jnp.sum(both, axis=0, keepdims=True)
        return total

    gain_sum = lax.fori_loop(0, 4, weighted, jnp.zeros((1, PAIR), F32))
    sy_own[:, :PAIR] = gain_sum / gain_ref[:, pl.ds(pl.multiple_of(me * PAIR, HD), PAIR)]
    small_y = [send(sy_own, sy.at[y], on_y(plus(y, dy, NY), c)) for dy in (1, 2, 3)]
    sy[y] = sy_own[...]

    for k in (1, 3, 2):
        spread_beside(k, 0)
        spread_beside(k, 1)

    def with_block(i, row_sum):
        from_x, from_y = plus(x, NX - lax.div(i, 2), NX), plus(yh, lax.rem(i, 2), 2)
        j = from_x * 2 + from_y
        columns = pl.ds(pl.multiple_of(j * PAIR, HD), PAIR)
        weights = wf[from_x, from_y].reshape(PAIR, KV)
        value[...] += dot(hid[j], weights, ((1,), (0,)))
        back = dot(vgb[...], weights, ((1,), (1,))).astype(BF16)
        hgrad[j] = back
        wide = back.astype(F32) * (xv[:, columns].astype(F32) * inv_ref[:, :1])
        return row_sum + lane_tiles(wide * gain_ref[:, columns])

    value[...] = jnp.zeros_like(value)
    row_sum = lax.fori_loop(0, 2, with_block, jnp.zeros((ROWS, HD), F32))

    for copy in small_y:
        copy.wait_recv()
    sz_own[...] = jnp.sum(sy[...], axis=0)
    small_z = []
    for dz in range(1, NZ):
        small_z.append(send(sz_own, sz.at[z], place(x, yh, c, plus(z, dz, NZ), yl)))
    sz[z] = sz_own[...]

    pl.when(c == 1)(sum_y)

    for copy in beside.values():
        copy.wait_recv()
    row_sum = lax.fori_loop(2, BLOCKS, with_block, row_sum)

    value_b = (value[...] + bias_ref[...]).astype(BF16)
    for g in range(GROUPS):
        mixed = dot(prob[g], value_b[:, g * HD : (g + 1) * HD], ((1,), (0,))).astype(BF16)
        for i in range(PER_GROUP):
            h = g * PER_GROUP + i
            att[:, h * HD : (h + 1) * HD] = mixed[i * ROWS : (i + 1) * ROWS]
    att_out = pltpu.make_async_copy(att, att_any, local_sem.at[8])
    att_out.start()

    mean = jnp.sum(row_sum, axis=1, keepdims=True) * (1.0 / D)

    def inputs_gradient(j, carry):
        columns = pl.ds(pl.multiple_of(j * PAIR, HD), PAIR)
        inverse = inv_ref[:, :1]
        normed = xv[:, columns].astype(F32) * inverse
        scaled = hgrad[j].astype(F32) * gain_ref[:, columns]
        gi[:, columns] = (inverse * (scaled - normed * mean)).astype(BF16)
        return carry

    lax.fori_loop(0, BLOCKS, inputs_gradient, 0)
    gi_out = pltpu.make_async_copy(gi, gi_any, local_sem.at[9])
    gi_out.start()

    for copy in small_z:
        copy.wait_recv()
    small_total = jnp.sum(sz[...], axis=0) * (1.0 / N_DP)
    sg_own[...] = small_total[:, :PAIR]
    gb_ref[...] = small_total[:, PAIR:]
    gathered = []
    for dx, dc in near:
        to = place(plus(x, dx, NX), yh, plus(c, dc, 2), z, yl)
        gathered.append(send(sg_own, sg.at[me], to))
    sg[me] = sg_own[...]

    for copy in columns_z:
        copy.wait_recv()
    over_z = zr[0].astype(F32)
    for i in range(1, NZ):
        over_z = over_z + zr[i].astype(F32)
    over_z = over_z * (1.0 / N_DP)
    gw_ref[...] = jnp.where(c == 0, over_z[:, :SHARE], over_z[:, WIDE - SHARE :])

    for copy in gathered:
        copy.wait_recv()
    gg_ref[...] = sg[...]

    for copy in sent + columns_z:
        copy.wait_send()
    for mine, there in crossing:

        @pl.when(jnp.logical_not(mine))
        def _():
            there.wait_send()

    att_out.wait()
    gi_out.wait()


def hand_over(
    att_in, gi_in, gw_in, gg_in, gb_in, att_out, gi_out, gw_out, gg_out, gb_out, att, gi, sem
):
    copies = []
    for i in range(PIECES):
        rows = pl.ds(i * (ROWS // PIECES), ROWS // PIECES)
        for source, held, out in ((gi_in, gi, gi_out), (att_in, att, att_out)):
            a, b = sem.at[0, len(copies)], sem.at[1, len(copies)]
            into = pltpu.make_async_copy(source.at[rows], held.at[rows], a)
            into.start()
            copies.append((into, pltpu.make_async_copy(held.at[rows], out.at[rows], b)))
    gw_out[...] = gw_in[...]
    gg_out[...] = gg_in[...]
    gb_out[...] = gb_in[...]
    for into, out in copies:
        into.wait()
        out.start()
    for into, out in copies:
        out.wait()


def local(inputs, queries, keys, doc_ids, grad_out, gain, bias, w_value):
    whole = pl.BlockSpec(memory_space=pltpu.VMEM)
    anywhere = pl.BlockSpec(memory_space=pl.ANY)
    summed = pl.pallas_call(
        kernel,
        out_shape=(
            jax.ShapeDtypeStruct((ROWS, QD), BF16),
            jax.ShapeDtypeStruct((ROWS, D), BF16),
            jax.ShapeDtypeStruct((COLUMNS, SHARE), F32),
            jax.ShapeDtypeStruct((BLOCKS, 1, PAIR), F32),
            jax.ShapeDtypeStruct((1, KV), F32),
        ),
        in_specs=[anywhere] * 4 + [whole] * 3 + [anywhere],
        out_specs=(anywhere, anywhere, whole, whole, whole),
        scratch_shapes=[
            pltpu.VMEM((ROWS, D), BF16),
            pltpu.VMEM((ROWS, QD), BF16),
            pltpu.VMEM((ROWS, KV), BF16),
            pltpu.VMEM((ROWS, QD), BF16),
            pltpu.VMEM((BLOCKS, ROWS, PAIR), BF16),
            pltpu.VMEM((ROWS, HD), F32),
            pltpu.VMEM((GROUPS, PER_GROUP * ROWS, ROWS), BF16),
            pltpu.VMEM((ROWS, KV), BF16),
            pltpu.VMEM((KV, 8 * ROWS), BF16),
            pltpu.VMEM((NX, 2, 2, 4, QUARTER, KV), BF16),
            pltpu.VMEM((8, ROWS, PAIR), BF16),
            pltpu.VMEM((ROWS, KV), F32),
            pltpu.VMEM((BLOCKS, ROWS, PAIR), BF16),
            pltpu.VMEM((ROWS, QD), BF16),
            pltpu.VMEM((ROWS, D), BF16),
            pltpu.VMEM((2, KV // 2, PAIR), BF16),
            pltpu.VMEM((NY, KV // 2, WIDE), BF16),
            pltpu.VMEM((NZ, COLUMNS, WIDE), BF16),
            pltpu.VMEM((NZ, COLUMNS, WIDE), BF16),
            pltpu.VMEM((1, SMALL), F32),
            pltpu.VMEM((NY, 1, SMALL), F32),
            pltpu.VMEM((1, SMALL), F32),
            pltpu.VMEM((NZ, 1, SMALL), F32),
            pltpu.VMEM((1, PAIR), F32),
            pltpu.VMEM((8, 1, PAIR), F32),
            pltpu.SemaphoreType.DMA((10,)),
            pltpu.SemaphoreType.DMA((COPIES,)),
            pltpu.SemaphoreType.DMA((COPIES,)),
            pltpu.SemaphoreType.REGULAR,
            pltpu.SemaphoreType.REGULAR,
        ],
        compiler_params=pltpu.CompilerParams(
            collective_id=0, has_side_effects=True, vmem_limit_bytes=60 * 1024 * 1024
        ),
    )(
        inputs, queries, keys, grad_out, doc_ids.reshape(1, ROWS), gain.reshape(1, D),
        bias.reshape(1, KV), w_value,
    )
    attention, grad_inputs, grad_w, grad_gain, grad_bias = pl.pallas_call(
        hand_over,
        out_shape=(
            jax.ShapeDtypeStruct((ROWS, QD), BF16),
            jax.ShapeDtypeStruct((ROWS, D), BF16),
            jax.ShapeDtypeStruct((COLUMNS, SHARE), F32),
            jax.ShapeDtypeStruct((BLOCKS, 1, PAIR), F32),
            jax.ShapeDtypeStruct((1, KV), F32),
        ),
        in_specs=[anywhere, anywhere, whole, whole, whole],
        out_specs=(anywhere, anywhere, whole, whole, whole),
        scratch_shapes=[
            pltpu.VMEM((ROWS, QD), BF16),
            pltpu.VMEM((ROWS, D), BF16),
            pltpu.SemaphoreType.DMA((2, 2 * PIECES)),
        ],
        compiler_params=pltpu.CompilerParams(vmem_limit_bytes=60 * 1024 * 1024),
    )(*summed)
    return attention, grad_inputs, grad_w.T, grad_gain.reshape(D), grad_bias.reshape(KV)


def solution(mesh):
    placed = (
        P(("blk", "dp"), None),
        P(("blk", "dp"), None),
        P(("blk", "dp"), None),
        P(("blk", "dp")),
        P(("blk", "dp"), None),
        P(),
        P(),
        P("blk", None),
    )
    return jax.shard_map(
        local,
        mesh=mesh,
        in_specs=placed,
        out_specs=(P(("blk", "dp"), None), P(("blk", "dp"), None), P("blk", "dp"), P(), P()),
        check_vma=False,
    )
```

```python
import math

import jax
import jax.numpy as jnp
from jax import lax
from jax.experimental import pallas as pl
from jax.experimental.pallas import tpu as pltpu
from jax.sharding import PartitionSpec as P

MESH = pl.DeviceIdType.MESH
F32, BF16 = jnp.float32, jnp.bfloat16

D = 5120
HD = 128
ROWS = 128
GROUPS = 4
PER_GROUP = 5
KV = GROUPS * HD
QD = KV * PER_GROUP
NX, NY, NZ = 4, 4, 16
SHARE = 320
QUARTER = SHARE // 4
PAIR = 2 * SHARE
BLOCKS = D // PAIR
WIDE = 384
COLUMNS = 16
SMALL = PAIR + KV
N_DP = 32
COPIES = 120
FAR_FIRST = (8, 7, 9, 6, 10, 5, 11, 4, 12, 3, 13, 2, 14, 1, 15)


def dot(a, b, dims):
    return lax.dot_general(a, b, (dims, ((), ())), preferred_element_type=F32)


def lane_tiles(a):
    total = a[:, :HD]
    for i in range(1, a.shape[1] // HD):
        total = total + a[:, i * HD : (i + 1) * HD]
    return total


def kernel(
    x_any, q_any, k_any, go_any, doc_any, gain_any, bias_any, w_any,
    att, gi, gw_ref, gg_ref, gb_ref,
    xv, qv, kv, gov, doc_ref, gain_ref, bias_ref, hid, inv_ref, prob, vgb, vt, wf, xh, value,
    hgrad, pt, yr, zs, zr, sy_own, sy, sz_own, sz, sg_own, sg,
    local_sem, send_sem, recv_sem, lower_sem, upper_sem,
):
    blk, dp = lax.axis_index("blk"), lax.axis_index("dp")
    x, yh, c = lax.div(blk, 4), lax.rem(lax.div(blk, 2), 2), lax.rem(blk, 2)
    z, yl = lax.div(dp, 2), lax.rem(dp, 2)
    y, half = yh * 2 + yl, lax.rem(z, 2)
    me = x * 2 + c

    def place(x, yh, c, z, yl):
        return (x * 4 + yh * 2 + c, z * 2 + yl)

    def on_y(y, c):
        return place(x, lax.div(y, 2), c, z, lax.rem(y, 2))

    def plus(a, by, n):
        return lax.rem(a + by, n)

    used = [0]

    def take(n):
        used[0] += n
        return used[0] - n

    def remote(src, dst, to, sent_at, received_at):
        return pltpu.make_async_remote_copy(
            src_ref=src,
            dst_ref=dst,
            send_sem=send_sem.at[sent_at],
            recv_sem=recv_sem.at[received_at],
            device_id=to,
            device_id_type=MESH,
        )

    sent = []

    def send(src, dst, to):
        i = take(1)
        copy = remote(src, dst, to, i, i)
        copy.start()
        sent.append(copy)
        return copy

    def pass_on(ref, to):
        return send(ref, ref, to)

    loads = [
        pltpu.make_async_copy(x_any, xv, local_sem.at[0]),
        pltpu.make_async_copy(q_any, qv, local_sem.at[1]),
        pltpu.make_async_copy(k_any, kv, local_sem.at[2]),
        pltpu.make_async_copy(go_any, gov, local_sem.at[3]),
        pltpu.make_async_copy(doc_any, doc_ref, local_sem.at[8]),
        pltpu.make_async_copy(bias_any, bias_ref, local_sem.at[9]),
        pltpu.make_async_copy(gain_any, gain_ref, local_sem.at[10]),
    ]
    loads += [
        pltpu.make_async_copy(
            w_any.at[pl.ds(i * QUARTER, QUARTER)], wf.at[x, yh, c, i], local_sem.at[4 + i]
        )
        for i in range(4)
    ]
    for copy in loads:
        copy.start()

    near = [(dx, dc) for dx in (2, 1, 3, 0) for dc in (0, 1) if (dx, dc) != (0, 0)]
    sibling = place(x, yh, 1 - c, z, yl)
    up = place(x, yh, c, plus(z, 1, NZ), yl)
    down = place(x, yh, c, plus(z, NZ - 1, NZ), yl)

    barrier = pltpu.get_barrier_semaphore()
    partners = [place(plus(x, dx, NX), yh, plus(c, dc, 2), z, yl) for dx, dc in near]
    partners += [on_y(plus(y, dy, NY), plus(c, dc, 2)) for dy in (1, 2, 3) for dc in (0, 1)]
    partners += [up, down]
    for partner in partners:
        pl.semaphore_signal(barrier, inc=1, device_id=partner, device_id_type=MESH)

    pl.semaphore_wait(barrier, len(partners))

    rounds = [0]

    def relay():
        if rounds[0] > 0:
            pl.semaphore_wait(lower_sem, 1)
            pl.semaphore_wait(upper_sem, 1)
        if rounds[0] < NZ // 2 - 1:
            pl.semaphore_signal(lower_sem, inc=1, device_id=up, device_id_type=MESH)
            pl.semaphore_signal(upper_sem, inc=1, device_id=down, device_id_type=MESH)
        rounds[0] += 1

    relay()

    def quarter(k, y_hi, y_lo):
        return wf.at[plus(x, NX - k, NX), y_hi, c, half * 2 + y_lo]

    def half_block(k, y_hi, h):
        return wf.at[plus(x, NX - k, NX), y_hi, c, pl.ds(h * 2, 2)]

    for copy in loads[7:]:
        copy.wait()
    along_x, along_y, along_z, beside = {}, {}, {}, {}

    others = (
        place(x, yh, c, z, 1 - yl),
        place(x, 1 - yh, c, z, yl),
        place(x, 1 - yh, c, z, 1 - yl),
    )

    def spread_y(k):
        for i in range(1 if k == 0 else 0, 3):
            along_y[k, i] = pass_on(quarter(k, yh, yl), others[i])

    def spread_z(k, other, is_up):
        y_hi = 1 - yh if other else yh
        along_z[other, k] = pass_on(half_block(k, y_hi, half), up if is_up else down)
        beside[other, k, 0] = pass_on(half_block(k, y_hi, half), sibling)

    def spread_beside(k, other):
        along_z[other, k].wait_recv()
        y_hi = 1 - yh if other else yh
        beside[other, k, 1] = pass_on(half_block(k, y_hi, 1 - half), sibling)

    spread_y(0)
    beside[0, 0, 0] = pass_on(half_block(0, yh, 0), sibling)
    beside[0, 0, 1] = pass_on(half_block(0, yh, 1), sibling)
    for k in (2, 1, 3):
        along_x[k] = pass_on(quarter(0, yh, yl), place(plus(x, k, NX), yh, c, z, yl))

    loads[0].wait()
    loads[6].wait()

    def squares(j, total):
        part = xv[:, pl.ds(pl.multiple_of(j * PAIR, HD), PAIR)].astype(F32)
        return total + lane_tiles(part * part)

    total = lax.fori_loop(0, BLOCKS, squares, jnp.zeros((ROWS, HD), F32))
    inverse = lax.rsqrt(jnp.sum(total, axis=1, keepdims=True) * (1.0 / D) + 1e-06)
    inv_ref[...] = jnp.broadcast_to(inverse, (ROWS, HD))

    def normalise(j, carry):
        columns = pl.ds(pl.multiple_of(j * PAIR, HD), PAIR)
        normed = xv[:, columns].astype(F32) * inv_ref[:, :1]
        hid[j] = (normed * gain_ref[:, columns]).astype(BF16)
        return carry

    lax.fori_loop(0, BLOCKS, normalise, 0)

    def send_hidden(first, width):
        columns = pl.ds(first, width)
        copies = []
        for dx, dc in near:
            to_x, to_c = plus(x, dx, NX), plus(c, dc, 2)
            src, dst = hid.at[to_x * 2 + to_c, :, columns], xh.at[me, :, columns]
            copies.append(send(src, dst, place(to_x, yh, to_c, z, yl)))
        return copies

    hidden_a = send_hidden(0, WIDE)
    xh[me] = hid[me]

    for copy in loads[1:6]:
        copy.wait()
    doc_row = jnp.broadcast_to(doc_ref[...].astype(F32), (ROWS, ROWS))
    positions = lax.broadcasted_iota(jnp.int32, (ROWS, ROWS), 0)
    key_positions = lax.broadcasted_iota(jnp.int32, (ROWS, ROWS), 1)
    allowed = (positions >= key_positions) & (doc_row == doc_row.T)

    def stacked(ref, g):
        heads = range(g * PER_GROUP, (g + 1) * PER_GROUP)
        return jnp.concatenate([ref[:, h * HD : (h + 1) * HD] for h in heads], axis=0)

    for g in range(GROUPS):
        group = slice(g * HD, (g + 1) * HD)
        scores = dot(stacked(qv, g), kv[:, group], ((1,), (1,))) * (1.0 / math.sqrt(HD))
        scores = jnp.where(allowed[None], scores.reshape(PER_GROUP, ROWS, ROWS), -1e30)
        exponent = jnp.exp(scores - jnp.max(scores, axis=-1, keepdims=True))
        chances = exponent / jnp.sum(exponent, axis=-1, keepdims=True)
        chances = chances.reshape(PER_GROUP * ROWS, ROWS).astype(BF16)
        prob[g] = chances
        value_grad = dot(chances, stacked(gov, g), ((0,), (0,)))
        vgb[:, group] = value_grad.astype(BF16)
        vt[group, pl.ds(pl.multiple_of(me * HD, HD), HD)] = value_grad.T.astype(BF16)

    def turned(x, c):
        return vt.at[:, pl.ds(pl.multiple_of((x * 2 + c) * HD, HD), HD)]

    turned_x = {}
    for k in (2, 1, 3):
        turned_x[k] = pass_on(turned(x, c), place(plus(x, k, NX), yh, c, z, yl))
    turned_beside = [pass_on(turned(x, c), sibling)]
    relay()

    for i in (1, 2):
        along_y[0, i].wait_recv()
    spread_z(0, 1, True)
    relay()
    for k in (1, 3, 2):
        along_x[k].wait_recv()
        spread_y(k)
    relay()
    spread_beside(0, 1)
    relay()
    for copy in hidden_a:
        copy.wait_recv()
    hidden_b = send_hidden(WIDE, PAIR - WIDE)
    for k in (1, 3, 2):
        for i in range(3):
            along_y[k, i].wait_recv()
        spread_z(k, 0, k != 3)
        spread_z(k, 1, k == 3)
    relay()

    for k in (1, 3, 2):
        turned_x[k].wait_recv()
        turned_beside.append(pass_on(turned(plus(x, NX - k, NX), c), sibling))
    relay()

    def product(first, width):
        def step(i, carry):
            rows = pl.ds(pl.multiple_of(i * 128, 128), 128)
            columns = slice(first, first + width)
            part = dot(vt[rows, :], xh[:, :, columns].reshape(8 * ROWS, width), ((1,), (0,)))
            part = part.astype(BF16).reshape(4, 2, COLUMNS, width)
            to = pl.ds(pl.multiple_of(i * 64, 64), 64)
            pt[0, to, columns] = part[:, 0].reshape(64, width)
            pt[1, to, columns] = part[:, 1].reshape(64, width)
            return carry

        lax.fori_loop(0, 4, step, 0)

    y_sent, y_received = take(4), used[0] - 4
    crossing = []

    def send_y(to_c):
        for side in (0, 1):
            to_y = 2 * c + side
            src, dst = pt.at[side, :, pl.ds(to_c * 256, WIDE)], yr.at[y]
            mine = (to_y == y) & (c == to_c)
            there = remote(src, dst, on_y(to_y, to_c), y_sent + side * 2 + to_c, y_received + y)
            here = pltpu.make_async_copy(src, dst, recv_sem.at[y_received + y])
            crossing.append((mine, there))

            @pl.when(mine)
            def _():
                here.start()

            @pl.when(jnp.logical_not(mine))
            def _():
                there.start()

    z_first = take(NZ - 1)
    columns_z = []
    for dz in FAR_FIRST:
        to_z = plus(z, dz, NZ)
        i = z_first + dz - 1
        columns_z.append(remote(zs.at[to_z], zr.at[z], place(x, yh, c, to_z, yl), i, i))

    def sum_y():
        for i in range(NY):
            pltpu.make_async_copy(yr.at[i], yr.at[i], recv_sem.at[y_received + i]).wait()
        over_y = yr[0].astype(F32)
        for i in range(1, NY):
            over_y = over_y + yr[i].astype(F32)
        zs[...] = over_y.astype(BF16).reshape(NZ, COLUMNS, WIDE)
        for copy in columns_z:
            copy.start()
        zr[z] = zs[z]

    for copy in turned_beside:
        copy.wait_recv()
    product(0, WIDE)
    send_y(0)
    relay()
    for copy in hidden_b:
        copy.wait_recv()
    product(WIDE, PAIR - WIDE)
    send_y(1)

    for key in ((0, 0, 0), (0, 0, 1), (1, 0, 0), (1, 0, 1)):
        beside.pop(key).wait_recv()
    ones = jnp.ones((8, 8 * ROWS), BF16)
    sy_own[:, PAIR:] = dot(ones, vt[...], ((1,), (1,)))[:1]

    def weighted(i, total):
        columns = pl.ds(pl.multiple_of(i * 128, 128), 128)
        turned_w = wf[x, c, :, :, :, columns].reshape(PAIR, 128).astype(F32).T
        turned_w = turned_w.reshape(4, 2, COLUMNS, PAIR)
        rows = pl.ds(pl.multiple_of(i * 64, 64), 64)
        for side in (0, 1):
            both = pt[side, rows, :].astype(F32) * turned_w[:, side].reshape(64, PAIR)
            total = total + jnp.sum(both, axis=0, keepdims=True)
        return total

    gain_sum = lax.fori_loop(0, 4, weighted, jnp.zeros((1, PAIR), F32))
    sy_own[:, :PAIR] = gain_sum / gain_ref[:, pl.ds(pl.multiple_of(me * PAIR, HD), PAIR)]
    small_y = [send(sy_own, sy.at[y], on_y(plus(y, dy, NY), c)) for dy in (1, 2, 3)]
    sy[y] = sy_own[...]
    pl.when(c == 0)(sum_y)

    for k in (1, 3, 2):
        spread_beside(k, 0)
        spread_beside(k, 1)

    def with_block(i, row_sum):
        from_x, from_y = plus(x, NX - lax.div(i, 2), NX), plus(yh, lax.rem(i, 2), 2)
        j = from_x * 2 + from_y
        columns = pl.ds(pl.multiple_of(j * PAIR, HD), PAIR)
        weights = wf[from_x, from_y].reshape(PAIR, KV)
        value[...] += dot(hid[j], weights, ((1,), (0,)))
        back = dot(vgb[...], weights, ((1,), (1,))).astype(BF16)
        hgrad[j] = back
        wide = back.astype(F32) * (xv[:, columns].astype(F32) * inv_ref[:, :1])
        return row_sum + lane_tiles(wide * gain_ref[:, columns])

    value[...] = jnp.zeros_like(value)
    row_sum = lax.fori_loop(0, 2, with_block, jnp.zeros((ROWS, HD), F32))

    for copy in small_y:
        copy.wait_recv()
    sz_own[...] = jnp.sum(sy[...], axis=0)
    small_z = []
    for dz in FAR_FIRST:
        small_z.append(send(sz_own, sz.at[z], place(x, yh, c, plus(z, dz, NZ), yl)))
    sz[z] = sz_own[...]

    pl.when(c == 1)(sum_y)

    for copy in beside.values():
        copy.wait_recv()
    row_sum = lax.fori_loop(2, BLOCKS, with_block, row_sum)

    value_b = (value[...] + bias_ref[...]).astype(BF16)
    for g in range(GROUPS):
        mixed = dot(prob[g], value_b[:, g * HD : (g + 1) * HD], ((1,), (0,))).astype(BF16)
        for i in range(PER_GROUP):
            h = g * PER_GROUP + i
            att[:, h * HD : (h + 1) * HD] = mixed[i * ROWS : (i + 1) * ROWS]

    mean = jnp.sum(row_sum, axis=1, keepdims=True) * (1.0 / D)

    def inputs_gradient(j, carry):
        columns = pl.ds(pl.multiple_of(j * PAIR, HD), PAIR)
        inverse = inv_ref[:, :1]
        normed = xv[:, columns].astype(F32) * inverse
        scaled = hgrad[j].astype(F32) * gain_ref[:, columns]
        gi[:, columns] = (inverse * (scaled - normed * mean)).astype(BF16)
        return carry

    lax.fori_loop(0, BLOCKS, inputs_gradient, 0)

    for copy in small_z:
        copy.wait_recv()
    small_total = jnp.sum(sz[...], axis=0) * (1.0 / N_DP)
    sg_own[...] = small_total[:, :PAIR]
    gb_ref[...] = small_total[:, PAIR:]
    gathered = []
    for dx, dc in near:
        to = place(plus(x, dx, NX), yh, plus(c, dc, 2), z, yl)
        gathered.append(send(sg_own, sg.at[me], to))
    sg[me] = sg_own[...]

    for copy in columns_z:
        copy.wait_recv()
    over_z = zr[0].astype(F32)
    for i in range(1, NZ):
        over_z = over_z + zr[i].astype(F32)
    over_z = over_z * (1.0 / N_DP)
    gw_ref[...] = jnp.where(c == 0, over_z[:, :SHARE], over_z[:, WIDE - SHARE :])

    for copy in gathered:
        copy.wait_recv()
    gg_ref[...] = sg[...]

    for copy in sent + columns_z:
        copy.wait_send()
    for mine, there in crossing:

        @pl.when(jnp.logical_not(mine))
        def _():
            there.wait_send()


def hand_over(*refs):
    results, outs, sem = refs[:5], refs[5:10], refs[10]
    copies = [pltpu.make_async_copy(results[i], outs[i], sem.at[i]) for i in range(5)]
    for copy in copies:
        copy.start()
    for copy in copies:
        copy.wait()


def local(inputs, queries, keys, doc_ids, grad_out, gain, bias, w_value):
    whole = pl.BlockSpec(memory_space=pltpu.VMEM)
    anywhere = pl.BlockSpec(memory_space=pl.ANY)
    arguments = (
        inputs, queries, keys, grad_out, doc_ids.reshape(1, ROWS), gain.reshape(1, D),
        bias.reshape(1, KV), w_value,
    )
    summed = pl.pallas_call(
        kernel,
        out_shape=(
            pltpu.VMEM((ROWS, QD), BF16),
            pltpu.VMEM((ROWS, D), BF16),
            pltpu.VMEM((COLUMNS, SHARE), F32),
            pltpu.VMEM((BLOCKS, 1, PAIR), F32),
            pltpu.VMEM((1, KV), F32),
        ),
        in_specs=[anywhere] * len(arguments),
        out_specs=(whole,) * 5,
        scratch_shapes=[
            pltpu.VMEM((ROWS, D), BF16),
            pltpu.VMEM((ROWS, QD), BF16),
            pltpu.VMEM((ROWS, KV), BF16),
            pltpu.VMEM((ROWS, QD), BF16),
            pltpu.VMEM((1, ROWS), jnp.int32),
            pltpu.VMEM((1, D), F32),
            pltpu.VMEM((1, KV), F32),
            pltpu.VMEM((BLOCKS, ROWS, PAIR), BF16),
            pltpu.VMEM((ROWS, HD), F32),
            pltpu.VMEM((GROUPS, PER_GROUP * ROWS, ROWS), BF16),
            pltpu.VMEM((ROWS, KV), BF16),
            pltpu.VMEM((KV, 8 * ROWS), BF16),
            pltpu.VMEM((NX, 2, 2, 4, QUARTER, KV), BF16),
            pltpu.VMEM((8, ROWS, PAIR), BF16),
            pltpu.VMEM((ROWS, KV), F32),
            pltpu.VMEM((BLOCKS, ROWS, PAIR), BF16),
            pltpu.VMEM((2, KV // 2, PAIR), BF16),
            pltpu.VMEM((NY, KV // 2, WIDE), BF16),
            pltpu.VMEM((NZ, COLUMNS, WIDE), BF16),
            pltpu.VMEM((NZ, COLUMNS, WIDE), BF16),
            pltpu.VMEM((1, SMALL), F32),
            pltpu.VMEM((NY, 1, SMALL), F32),
            pltpu.VMEM((1, SMALL), F32),
            pltpu.VMEM((NZ, 1, SMALL), F32),
            pltpu.VMEM((1, PAIR), F32),
            pltpu.VMEM((8, 1, PAIR), F32),
            pltpu.SemaphoreType.DMA((11,)),
            pltpu.SemaphoreType.DMA((COPIES,)),
            pltpu.SemaphoreType.DMA((COPIES,)),
            pltpu.SemaphoreType.REGULAR,
            pltpu.SemaphoreType.REGULAR,
        ],
        compiler_params=pltpu.CompilerParams(
            collective_id=0, has_side_effects=True, vmem_limit_bytes=32 * 1024 * 1024
        ),
    )(
        *(pltpu.with_memory_space_constraint(argument, pltpu.HBM) for argument in arguments)
    )
    attention, grad_inputs, grad_w, grad_gain, grad_bias = pl.pallas_call(
        hand_over,
        out_shape=(
            jax.ShapeDtypeStruct((ROWS, QD), BF16),
            jax.ShapeDtypeStruct((ROWS, D), BF16),
            jax.ShapeDtypeStruct((COLUMNS, SHARE), F32),
            jax.ShapeDtypeStruct((BLOCKS, 1, PAIR), F32),
            jax.ShapeDtypeStruct((1, KV), F32),
        ),
        in_specs=[whole] * 5,
        out_specs=(anywhere,) * 5,
        scratch_shapes=[pltpu.SemaphoreType.DMA((5,))],
        compiler_params=pltpu.CompilerParams(vmem_limit_bytes=16 * 1024 * 1024),
    )(*summed)
    return attention, grad_inputs, grad_w.T, grad_gain.reshape(D), grad_bias.reshape(KV)


def solution(mesh):
    placed = (
        P(("blk", "dp"), None),
        P(("blk", "dp"), None),
        P(("blk", "dp"), None),
        P(("blk", "dp")),
        P(("blk", "dp"), None),
        P(),
        P(),
        P("blk", None),
    )
    return jax.shard_map(
        local,
        mesh=mesh,
        in_specs=placed,
        out_specs=(P(("blk", "dp"), None), P(("blk", "dp"), None), P("blk", "dp"), P(), P()),
        check_vma=False,
    )
```

```python
import math

import jax
import jax.numpy as jnp
from jax import lax
from jax.experimental import pallas as pl
from jax.experimental.pallas import tpu as pltpu
from jax.sharding import PartitionSpec as P

MESH = pl.DeviceIdType.MESH
F32, BF16 = jnp.float32, jnp.bfloat16

D = 5120
HD = 128
ROWS = 128
GROUPS = 4
PER_GROUP = 5
KV = GROUPS * HD
QD = KV * PER_GROUP
NX, NY, NZ = 4, 4, 16
SHARE = 320
QUARTER = SHARE // 4
PAIR = 2 * SHARE
BLOCKS = D // PAIR
WIDE = 384
COLUMNS = 16
SMALL = PAIR + HD
N_DP = 32
COPIES = 144
FAR_FIRST = (8, 7, 9, 6, 10, 5, 11, 4, 12, 3, 13, 2, 14, 1, 15)


def dot(a, b, dims):
    return lax.dot_general(a, b, (dims, ((), ())), preferred_element_type=F32)


def lane_tiles(a):
    total = a[:, :HD]
    for i in range(1, a.shape[1] // HD):
        total = total + a[:, i * HD : (i + 1) * HD]
    return total


def kernel(
    x_any, q_any, k_any, go_any, doc_any, gain_any, bias_any, w_any,
    att, gi, gw_ref, gg_ref, gb_ref,
    xv, qv, kv, gov, doc_ref, gain_ref, bias_ref, hid, inv_ref, prob, vgb, vt, wf, xh, value,
    hgrad, pt, yr, zs, zr, middle_own, middle_in, sz_own, sz, sg_own, sg,
    local_sem, send_sem, recv_sem, lower_sem, upper_sem,
):
    blk, dp = lax.axis_index("blk"), lax.axis_index("dp")
    x, yh, c = lax.div(blk, 4), lax.rem(lax.div(blk, 2), 2), lax.rem(blk, 2)
    z, yl = lax.div(dp, 2), lax.rem(dp, 2)
    y, half = yh * 2 + yl, lax.rem(z, 2)
    me = x * 2 + c

    def place(x, yh, c, z, yl):
        return (x * 4 + yh * 2 + c, z * 2 + yl)

    def on_y(y, c):
        return place(x, lax.div(y, 2), c, z, lax.rem(y, 2))

    def plus(a, by, n):
        return lax.rem(a + by, n)

    used = [0]

    def take(n):
        used[0] += n
        return used[0] - n

    def remote(src, dst, to, sent_at, received_at):
        return pltpu.make_async_remote_copy(
            src_ref=src,
            dst_ref=dst,
            send_sem=send_sem.at[sent_at],
            recv_sem=recv_sem.at[received_at],
            device_id=to,
            device_id_type=MESH,
        )

    sent = []

    def send(src, dst, to):
        i = take(1)
        copy = remote(src, dst, to, i, i)
        copy.start()
        sent.append(copy)
        return copy

    def pass_on(ref, to):
        return send(ref, ref, to)

    loads = [
        pltpu.make_async_copy(x_any, xv, local_sem.at[0]),
        pltpu.make_async_copy(q_any, qv, local_sem.at[1]),
        pltpu.make_async_copy(k_any, kv, local_sem.at[2]),
        pltpu.make_async_copy(go_any, gov, local_sem.at[3]),
        pltpu.make_async_copy(doc_any, doc_ref, local_sem.at[8]),
        pltpu.make_async_copy(bias_any, bias_ref, local_sem.at[9]),
        pltpu.make_async_copy(gain_any, gain_ref, local_sem.at[10]),
    ]
    loads += [
        pltpu.make_async_copy(
            w_any.at[pl.ds(i * QUARTER, QUARTER)], wf.at[x, yh, c, i], local_sem.at[4 + i]
        )
        for i in range(4)
    ]
    for copy in loads:
        copy.start()

    near = [(dx, dc) for dx in (2, 1, 3, 0) for dc in (0, 1) if (dx, dc) != (0, 0)]
    sibling = place(x, yh, 1 - c, z, yl)
    up = place(x, yh, c, plus(z, 1, NZ), yl)
    down = place(x, yh, c, plus(z, NZ - 1, NZ), yl)

    barrier = pltpu.get_barrier_semaphore()
    partners = [place(plus(x, dx, NX), yh, plus(c, dc, 2), z, yl) for dx, dc in near]
    partners += [on_y(plus(y, dy, NY), plus(c, dc, 2)) for dy in (1, 2, 3) for dc in (0, 1)]
    partners += [up, down]
    for partner in partners:
        pl.semaphore_signal(barrier, inc=1, device_id=partner, device_id_type=MESH)

    pl.semaphore_wait(barrier, len(partners))

    rounds = [0]

    def relay():
        if rounds[0] > 0:
            pl.semaphore_wait(lower_sem, 1)
            pl.semaphore_wait(upper_sem, 1)
        if rounds[0] < NZ // 2 - 1:
            pl.semaphore_signal(lower_sem, inc=1, device_id=up, device_id_type=MESH)
            pl.semaphore_signal(upper_sem, inc=1, device_id=down, device_id_type=MESH)
        rounds[0] += 1

    relay()

    def quarter(k, y_hi, y_lo):
        return wf.at[plus(x, NX - k, NX), y_hi, c, half * 2 + y_lo]

    def half_block(k, y_hi, h):
        return wf.at[plus(x, NX - k, NX), y_hi, c, pl.ds(h * 2, 2)]

    for copy in loads[7:]:
        copy.wait()
    along_x, along_y, along_z, beside = {}, {}, {}, {}

    others = (
        place(x, yh, c, z, 1 - yl),
        place(x, 1 - yh, c, z, yl),
        place(x, 1 - yh, c, z, 1 - yl),
    )

    def spread_y(k):
        for i in range(1 if k == 0 else 0, 3):
            along_y[k, i] = pass_on(quarter(k, yh, yl), others[i])

    def spread_z(k, other, is_up):
        y_hi = 1 - yh if other else yh
        along_z[other, k] = pass_on(half_block(k, y_hi, half), up if is_up else down)
        beside[other, k, 0] = pass_on(half_block(k, y_hi, half), sibling)

    def spread_beside(k, other):
        along_z[other, k].wait_recv()
        y_hi = 1 - yh if other else yh
        beside[other, k, 1] = pass_on(half_block(k, y_hi, 1 - half), sibling)

    spread_y(0)
    beside[0, 0, 0] = pass_on(half_block(0, yh, 0), sibling)
    beside[0, 0, 1] = pass_on(half_block(0, yh, 1), sibling)
    for k in (2, 1, 3):
        along_x[k] = pass_on(quarter(0, yh, yl), place(plus(x, k, NX), yh, c, z, yl))

    loads[0].wait()
    loads[6].wait()

    def squares(j, total):
        part = xv[:, pl.ds(pl.multiple_of(j * PAIR, HD), PAIR)].astype(F32)
        return total + lane_tiles(part * part)

    total = lax.fori_loop(0, BLOCKS, squares, jnp.zeros((ROWS, HD), F32))
    inverse = lax.rsqrt(jnp.sum(total, axis=1, keepdims=True) * (1.0 / D) + 1e-06)
    inv_ref[...] = jnp.broadcast_to(inverse, (ROWS, HD))

    def normalise(j, carry):
        columns = pl.ds(pl.multiple_of(j * PAIR, HD), PAIR)
        normed = xv[:, columns].astype(F32) * inv_ref[:, :1]
        hid[j] = (normed * gain_ref[:, columns]).astype(BF16)
        return carry

    lax.fori_loop(0, BLOCKS, normalise, 0)

    def send_hidden(first, width):
        columns = pl.ds(first, width)
        copies = []
        for dx, dc in near:
            to_x, to_c = plus(x, dx, NX), plus(c, dc, 2)
            src, dst = hid.at[to_x * 2 + to_c, :, columns], xh.at[me, :, columns]
            copies.append(send(src, dst, place(to_x, yh, to_c, z, yl)))
        return copies

    hidden_a = send_hidden(0, WIDE)
    xh[me] = hid[me]

    for copy in loads[1:6]:
        copy.wait()
    doc_row = jnp.broadcast_to(doc_ref[...].astype(F32), (ROWS, ROWS))
    positions = lax.broadcasted_iota(jnp.int32, (ROWS, ROWS), 0)
    key_positions = lax.broadcasted_iota(jnp.int32, (ROWS, ROWS), 1)
    allowed = (positions >= key_positions) & (doc_row == doc_row.T)

    def stacked(ref, g):
        heads = range(g * PER_GROUP, (g + 1) * PER_GROUP)
        return jnp.concatenate([ref[:, h * HD : (h + 1) * HD] for h in heads], axis=0)

    for g in range(GROUPS):
        group = slice(g * HD, (g + 1) * HD)
        scores = dot(stacked(qv, g), kv[:, group], ((1,), (1,))) * (1.0 / math.sqrt(HD))
        scores = jnp.where(allowed[None], scores.reshape(PER_GROUP, ROWS, ROWS), -1e30)
        exponent = jnp.exp(scores - jnp.max(scores, axis=-1, keepdims=True))
        chances = exponent / jnp.sum(exponent, axis=-1, keepdims=True)
        chances = chances.reshape(PER_GROUP * ROWS, ROWS).astype(BF16)
        prob[g] = chances
        value_grad = dot(chances, stacked(gov, g), ((0,), (0,)))
        vgb[:, group] = value_grad.astype(BF16)
        vt[group, pl.ds(pl.multiple_of(me * HD, HD), HD)] = value_grad.T.astype(BF16)

    def turned(x, c):
        return vt.at[:, pl.ds(pl.multiple_of((x * 2 + c) * HD, HD), HD)]

    turned_x = {}
    for k in (2, 1, 3):
        turned_x[k] = pass_on(turned(x, c), place(plus(x, k, NX), yh, c, z, yl))
    turned_beside = [pass_on(turned(x, c), sibling)]
    relay()

    for i in (1, 2):
        along_y[0, i].wait_recv()
    spread_z(0, 1, True)
    relay()
    for k in (1, 3, 2):
        along_x[k].wait_recv()
        spread_y(k)
    relay()
    spread_beside(0, 1)
    relay()
    for copy in hidden_a:
        copy.wait_recv()
    hidden_b = send_hidden(WIDE, PAIR - WIDE)
    for k in (1, 3, 2):
        for i in range(3):
            along_y[k, i].wait_recv()
        spread_z(k, 0, k != 3)
        spread_z(k, 1, k == 3)
    relay()

    for k in (1, 3, 2):
        turned_x[k].wait_recv()
        turned_beside.append(pass_on(turned(plus(x, NX - k, NX), c), sibling))
    relay()

    def product(first, width):
        def step(i, carry):
            rows = pl.ds(pl.multiple_of(i * 256, 256), 256)
            columns = slice(first, first + width)
            part = dot(vt[rows, :], xh[:, :, columns].reshape(8 * ROWS, width), ((1,), (0,)))
            part = part.astype(BF16).reshape(8, 2, COLUMNS, width)
            to = pl.ds(pl.multiple_of(i * 128, 128), 128)
            pt[0, to, columns] = part[:, 0].reshape(128, width)
            pt[1, to, columns] = part[:, 1].reshape(128, width)
            return carry

        lax.fori_loop(0, 2, step, 0)

    parts = ((0, WIDE), (WIDE, PAIR - WIDE))
    y_sent, y_received = take(4), used[0] - 4
    crossing = []

    def send_y(to_c):
        first, width = parts[to_c]
        for side in (0, 1):
            to_y = 2 * c + side
            src, dst = pt.at[side, :, pl.ds(first, width)], yr.at[y, :, pl.ds(0, width)]
            mine = (to_y == y) & (c == to_c)
            there = remote(src, dst, on_y(to_y, to_c), y_sent + side * 2 + to_c, y_received + y)
            here = pltpu.make_async_copy(src, dst, recv_sem.at[y_received + y])
            crossing.append((mine, there))

            @pl.when(mine)
            def _():
                here.start()

            @pl.when(jnp.logical_not(mine))
            def _():
                there.start()

    z_first = take(NZ - 1)

    def along_z_copies(width):
        copies = []
        for dz in FAR_FIRST:
            to_z = plus(z, dz, NZ)
            i = z_first + dz - 1
            src, dst = zs.at[to_z, :, pl.ds(0, width)], zr.at[z, :, pl.ds(0, width)]
            copies.append(remote(src, dst, place(x, yh, c, to_z, yl), i, i))
        return copies

    def sum_y(core):
        width = parts[core][1]
        for i in range(NY):
            arrived = yr.at[i, :, pl.ds(0, width)]
            pltpu.make_async_copy(arrived, arrived, recv_sem.at[y_received + i]).wait()
        over_y = yr[0, :, :width].astype(F32)
        for i in range(1, NY):
            over_y = over_y + yr[i, :, :width].astype(F32)
        zs[:, :, :width] = over_y.astype(BF16).reshape(NZ, COLUMNS, width)
        for copy in along_z_copies(width):
            copy.start()
        zr[z, :, :width] = zs[z, :, :width]

    def sum_z(core):
        width = parts[core][1]
        for copy in along_z_copies(width):
            copy.wait()
        over_z = zr[0, :, :width].astype(F32)
        for i in range(1, NZ):
            over_z = over_z + zr[i, :, :width].astype(F32)
        return over_z * (1.0 / N_DP)

    middle = take(1)

    def middle_copy():
        return remote(middle_own, middle_in, sibling, middle, middle)

    for copy in turned_beside:
        copy.wait_recv()
    product(0, WIDE)
    send_y(0)
    relay()

    for key in ((0, 0, 0), (0, 0, 1), (1, 0, 0), (1, 0, 1)):
        beside.pop(key).wait_recv()
    ones = jnp.ones((8, 8 * ROWS), BF16)
    one_head = pl.ds(pl.multiple_of(x * HD, HD), HD)
    sz_own[:, PAIR:] = dot(ones, vt[one_head, :], ((1,), (1,)))[:1]

    def weighted(first, width):
        lanes = slice(first, first + width)

        def step(i, total):
            columns = pl.ds(pl.multiple_of(i * 128, 128), 128)
            turned_w = wf[x, c, :, :, :, columns].reshape(PAIR, 128)[lanes].astype(F32).T
            turned_w = turned_w.reshape(4, 2, COLUMNS, width)
            rows = pl.ds(pl.multiple_of(i * 64, 64), 64)
            for side in (0, 1):
                both = pt[side, rows, lanes].astype(F32) * turned_w[:, side].reshape(64, width)
                total = total + jnp.sum(both, axis=0, keepdims=True)
            return total

        total = lax.fori_loop(0, 4, step, jnp.zeros((1, width), F32))
        own = pl.ds(pl.multiple_of(me * PAIR + first, HD), width)
        sz_own[:, lanes] = total / gain_ref[:, own]

    weighted(0, WIDE)

    for copy in hidden_b:
        copy.wait_recv()
    product(WIDE, PAIR - WIDE)
    send_y(1)
    weighted(WIDE, PAIR - WIDE)
    small_z = []
    for dz in FAR_FIRST:
        small_z.append(send(sz_own, sz.at[z], place(x, yh, c, plus(z, dz, NZ), yl)))
    sz[z] = sz_own[...]
    pl.when(c == 0)(lambda: sum_y(0))

    for k in (1, 3, 2):
        spread_beside(k, 0)
        spread_beside(k, 1)

    def with_block(i, row_sum):
        from_x, from_y = plus(x, NX - lax.div(i, 2), NX), plus(yh, lax.rem(i, 2), 2)
        j = from_x * 2 + from_y
        columns = pl.ds(pl.multiple_of(j * PAIR, HD), PAIR)
        weights = wf[from_x, from_y].reshape(PAIR, KV)
        value[...] += dot(hid[j], weights, ((1,), (0,)))
        back = dot(vgb[...], weights, ((1,), (1,))).astype(BF16)
        hgrad[j] = back
        wide = back.astype(F32) * (xv[:, columns].astype(F32) * inv_ref[:, :1])
        return row_sum + lane_tiles(wide * gain_ref[:, columns])

    value[...] = jnp.zeros_like(value)
    row_sum = lax.fori_loop(0, 2, with_block, jnp.zeros((ROWS, HD), F32))

    pl.when(c == 1)(lambda: sum_y(1))

    for copy in beside.values():
        copy.wait_recv()
    row_sum = lax.fori_loop(2, BLOCKS, with_block, row_sum)

    for copy in small_z:
        copy.wait_recv()
    sg_own[...] = jnp.sum(sz[...], axis=0) * (1.0 / N_DP)
    gathered = []
    for dy in (2, 1, 3, 0):
        for dx, dc in near + [(0, 0)]:
            if (dx, dy, dc) != (0, 0, 0):
                to_y = plus(y, dy, NY)
                to = place(
                    plus(x, dx, NX), lax.div(to_y, 2), plus(c, dc, 2), z, lax.rem(to_y, 2)
                )
                gathered.append(send(sg_own, sg.at[y * 8 + me], to))
    sg[y * 8 + me] = sg_own[...]

    value_b = (value[...] + bias_ref[...]).astype(BF16)
    for g in range(GROUPS):
        mixed = dot(prob[g], value_b[:, g * HD : (g + 1) * HD], ((1,), (0,))).astype(BF16)
        for i in range(PER_GROUP):
            h = g * PER_GROUP + i
            att[:, h * HD : (h + 1) * HD] = mixed[i * ROWS : (i + 1) * ROWS]

    mean = jnp.sum(row_sum, axis=1, keepdims=True) * (1.0 / D)

    def inputs_gradient(j, carry):
        columns = pl.ds(pl.multiple_of(j * PAIR, HD), PAIR)
        inverse = inv_ref[:, :1]
        normed = xv[:, columns].astype(F32) * inverse
        scaled = hgrad[j].astype(F32) * gain_ref[:, columns]
        gi[:, columns] = (inverse * (scaled - normed * mean)).astype(BF16)
        return carry

    lax.fori_loop(0, BLOCKS, inputs_gradient, 0)

    @pl.when(c == 0)
    def _():
        over_z = sum_z(0)
        gw_ref[...] = over_z[:, :SHARE]
        middle_own[...] = over_z[:, WIDE - HD :]
        middle_copy().start()


    @pl.when(c == 1)
    def _():
        over_z = sum_z(1)
        middle_copy().wait_recv()
        gw_ref[...] = jnp.concatenate([middle_in[:, HD // 2 :], over_z], axis=1)

    for copy in gathered:
        copy.wait_recv()
    over_all = jnp.sum(sg[...].reshape(NY, 8, 1, SMALL), axis=0)
    gg_ref[...] = over_all[:, :, :PAIR]
    for i in range(NX):
        gb_ref[:, i * HD : (i + 1) * HD] = over_all[2 * i, :, PAIR:]

    for copy in sent:
        copy.wait_send()

    @pl.when(c == 0)
    def _():
        middle_copy().wait_send()

    for mine, there in crossing:

        @pl.when(jnp.logical_not(mine))
        def _():
            there.wait_send()


def hand_over(*refs):
    results, outs, sem = refs[:5], refs[5:10], refs[10]
    copies = [pltpu.make_async_copy(results[i], outs[i], sem.at[i]) for i in range(5)]
    for copy in copies:
        copy.start()
    for copy in copies:
        copy.wait()


def local(inputs, queries, keys, doc_ids, grad_out, gain, bias, w_value):
    whole = pl.BlockSpec(memory_space=pltpu.VMEM)
    anywhere = pl.BlockSpec(memory_space=pl.ANY)
    arguments = (
        inputs, queries, keys, grad_out, doc_ids.reshape(1, ROWS), gain.reshape(1, D),
        bias.reshape(1, KV), w_value,
    )
    summed = pl.pallas_call(
        kernel,
        out_shape=(
            pltpu.VMEM((ROWS, QD), BF16),
            pltpu.VMEM((ROWS, D), BF16),
            pltpu.VMEM((COLUMNS, SHARE), F32),
            pltpu.VMEM((BLOCKS, 1, PAIR), F32),
            pltpu.VMEM((1, KV), F32),
        ),
        in_specs=[anywhere] * len(arguments),
        out_specs=(whole,) * 5,
        scratch_shapes=[
            pltpu.VMEM((ROWS, D), BF16),
            pltpu.VMEM((ROWS, QD), BF16),
            pltpu.VMEM((ROWS, KV), BF16),
            pltpu.VMEM((ROWS, QD), BF16),
            pltpu.VMEM((1, ROWS), jnp.int32),
            pltpu.VMEM((1, D), F32),
            pltpu.VMEM((1, KV), F32),
            pltpu.VMEM((BLOCKS, ROWS, PAIR), BF16),
            pltpu.VMEM((ROWS, HD), F32),
            pltpu.VMEM((GROUPS, PER_GROUP * ROWS, ROWS), BF16),
            pltpu.VMEM((ROWS, KV), BF16),
            pltpu.VMEM((KV, 8 * ROWS), BF16),
            pltpu.VMEM((NX, 2, 2, 4, QUARTER, KV), BF16),
            pltpu.VMEM((8, ROWS, PAIR), BF16),
            pltpu.VMEM((ROWS, KV), F32),
            pltpu.VMEM((BLOCKS, ROWS, PAIR), BF16),
            pltpu.VMEM((2, KV // 2, PAIR), BF16),
            pltpu.VMEM((NY, KV // 2, WIDE), BF16),
            pltpu.VMEM((NZ, COLUMNS, WIDE), BF16),
            pltpu.VMEM((NZ, COLUMNS, WIDE), BF16),
            pltpu.VMEM((COLUMNS, HD), F32),
            pltpu.VMEM((COLUMNS, HD), F32),
            pltpu.VMEM((1, SMALL), F32),
            pltpu.VMEM((NZ, 1, SMALL), F32),
            pltpu.VMEM((1, SMALL), F32),
            pltpu.VMEM((8 * NY, 1, SMALL), F32),
            pltpu.SemaphoreType.DMA((11,)),
            pltpu.SemaphoreType.DMA((COPIES,)),
            pltpu.SemaphoreType.DMA((COPIES,)),
            pltpu.SemaphoreType.REGULAR,
            pltpu.SemaphoreType.REGULAR,
        ],
        compiler_params=pltpu.CompilerParams(
            collective_id=0, has_side_effects=True, vmem_limit_bytes=32 * 1024 * 1024
        ),
    )(
        *(pltpu.with_memory_space_constraint(argument, pltpu.HBM) for argument in arguments)
    )
    attention, grad_inputs, grad_w, grad_gain, grad_bias = pl.pallas_call(
        hand_over,
        out_shape=(
            jax.ShapeDtypeStruct((ROWS, QD), BF16),
            jax.ShapeDtypeStruct((ROWS, D), BF16),
            jax.ShapeDtypeStruct((COLUMNS, SHARE), F32),
            jax.ShapeDtypeStruct((BLOCKS, 1, PAIR), F32),
            jax.ShapeDtypeStruct((1, KV), F32),
        ),
        in_specs=[whole] * 5,
        out_specs=(anywhere,) * 5,
        scratch_shapes=[pltpu.SemaphoreType.DMA((5,))],
        compiler_params=pltpu.CompilerParams(vmem_limit_bytes=16 * 1024 * 1024),
    )(*summed)
    return attention, grad_inputs, grad_w.T, grad_gain.reshape(D), grad_bias.reshape(KV)


def solution(mesh):
    placed = (
        P(("blk", "dp"), None),
        P(("blk", "dp"), None),
        P(("blk", "dp"), None),
        P(("blk", "dp")),
        P(("blk", "dp"), None),
        P(),
        P(),
        P("blk", None),
    )
    return jax.shard_map(
        local,
        mesh=mesh,
        in_specs=placed,
        out_specs=(P(("blk", "dp"), None), P(("blk", "dp"), None), P("blk", "dp"), P(), P()),
        check_vma=False,
    )
```

```python
import math

import jax
import jax.numpy as jnp
from jax import lax
from jax.experimental import pallas as pl
from jax.experimental.pallas import tpu as pltpu
from jax.sharding import PartitionSpec as P

MESH = pl.DeviceIdType.MESH
F32, BF16 = jnp.float32, jnp.bfloat16

D = 5120
HD = 128
ROWS = 128
GROUPS = 4
PER_GROUP = 5
KV = GROUPS * HD
QD = KV * PER_GROUP
NX, NY, NZ = 4, 4, 16
SHARE = 320
QUARTER = SHARE // 4
PAIR = 2 * SHARE
BLOCKS = D // PAIR
WIDE = 384
COLUMNS = 16
SMALL = PAIR + HD
N_DP = 32
COPIES = 144
FAR_FIRST = (8, 7, 9, 6, 10, 5, 11, 4, 12, 3, 13, 2, 14, 1, 15)


def dot(a, b, dims):
    return lax.dot_general(a, b, (dims, ((), ())), preferred_element_type=F32)


def lane_tiles(a):
    total = a[:, :HD]
    for i in range(1, a.shape[1] // HD):
        total = total + a[:, i * HD : (i + 1) * HD]
    return total


def kernel(
    x_any, q_any, k_any, go_any, doc_any, gain_any, bias_any, w_any,
    att, gi, gw_ref, gg_ref, gb_ref,
    xv, qv, kv, gov, doc_ref, gain_ref, bias_ref, hid, inv_ref, prob, vgb, vt, wf, xh, value,
    hgrad, pt, yr, zs, zr, middle_own, middle_in, sz_own, sz, sg_own, sg,
    local_sem, send_sem, recv_sem, lower_sem, upper_sem,
):
    blk, dp = lax.axis_index("blk"), lax.axis_index("dp")
    x, yh, c = lax.div(blk, 4), lax.rem(lax.div(blk, 2), 2), lax.rem(blk, 2)
    z, yl = lax.div(dp, 2), lax.rem(dp, 2)
    y, half = yh * 2 + yl, lax.rem(z, 2)
    me = x * 2 + c

    def place(x, yh, c, z, yl):
        return (x * 4 + yh * 2 + c, z * 2 + yl)

    def on_y(y, c):
        return place(x, lax.div(y, 2), c, z, lax.rem(y, 2))

    def plus(a, by, n):
        return lax.rem(a + by, n)

    used = [0]

    def take(n):
        used[0] += n
        return used[0] - n

    def remote(src, dst, to, sent_at, received_at):
        return pltpu.make_async_remote_copy(
            src_ref=src,
            dst_ref=dst,
            send_sem=send_sem.at[sent_at],
            recv_sem=recv_sem.at[received_at],
            device_id=to,
            device_id_type=MESH,
        )

    sent = []

    def send(src, dst, to):
        i = take(1)
        copy = remote(src, dst, to, i, i)
        copy.start()
        sent.append(copy)
        return copy

    def pass_on(ref, to):
        return send(ref, ref, to)

    loads = [
        pltpu.make_async_copy(x_any, xv, local_sem.at[0]),
        pltpu.make_async_copy(q_any, qv, local_sem.at[1]),
        pltpu.make_async_copy(k_any, kv, local_sem.at[2]),
        pltpu.make_async_copy(go_any, gov, local_sem.at[3]),
        pltpu.make_async_copy(doc_any, doc_ref, local_sem.at[8]),
        pltpu.make_async_copy(bias_any, bias_ref, local_sem.at[9]),
        pltpu.make_async_copy(gain_any, gain_ref, local_sem.at[10]),
    ]
    loads += [
        pltpu.make_async_copy(
            w_any.at[pl.ds(i * QUARTER, QUARTER)], wf.at[x, yh, c, i], local_sem.at[4 + i]
        )
        for i in range(4)
    ]
    for copy in loads:
        copy.start()

    near = [(dx, dc) for dx in (1, 3, 2, 0) for dc in (0, 1) if (dx, dc) != (0, 0)]
    sibling = place(x, yh, 1 - c, z, yl)
    up = place(x, yh, c, plus(z, 1, NZ), yl)
    down = place(x, yh, c, plus(z, NZ - 1, NZ), yl)

    barrier = pltpu.get_barrier_semaphore()
    partners = [place(plus(x, dx, NX), yh, plus(c, dc, 2), z, yl) for dx, dc in near]
    partners += [on_y(plus(y, dy, NY), plus(c, dc, 2)) for dy in (1, 2, 3) for dc in (0, 1)]
    partners += [up, down]
    for partner in partners:
        pl.semaphore_signal(barrier, inc=1, device_id=partner, device_id_type=MESH)

    pl.semaphore_wait(barrier, len(partners))

    rounds = [0]

    def relay():
        if rounds[0] > 0:
            pl.semaphore_wait(lower_sem, 1)
            pl.semaphore_wait(upper_sem, 1)
        if rounds[0] < NZ // 2 - 1:
            pl.semaphore_signal(lower_sem, inc=1, device_id=up, device_id_type=MESH)
            pl.semaphore_signal(upper_sem, inc=1, device_id=down, device_id_type=MESH)
        rounds[0] += 1

    relay()

    def quarter(k, y_hi, y_lo):
        return wf.at[plus(x, NX - k, NX), y_hi, c, half * 2 + y_lo]

    def half_block(k, y_hi, h):
        return wf.at[plus(x, NX - k, NX), y_hi, c, pl.ds(h * 2, 2)]

    for copy in loads[7:]:
        copy.wait()
    along_x, along_y, along_z, beside = {}, {}, {}, {}

    others = (
        place(x, yh, c, z, 1 - yl),
        place(x, 1 - yh, c, z, yl),
        place(x, 1 - yh, c, z, 1 - yl),
    )

    def spread_y(k):
        for i in range(1 if k == 0 else 0, 3):
            along_y[k, i] = pass_on(quarter(k, yh, yl), others[i])

    def spread_z(k, other, is_up):
        y_hi = 1 - yh if other else yh
        along_z[other, k] = pass_on(half_block(k, y_hi, half), up if is_up else down)
        beside[other, k, 0] = pass_on(half_block(k, y_hi, half), sibling)

    def spread_beside(k, other):
        along_z[other, k].wait_recv()
        y_hi = 1 - yh if other else yh
        beside[other, k, 1] = pass_on(half_block(k, y_hi, 1 - half), sibling)

    spread_y(0)
    beside[0, 0, 0] = pass_on(half_block(0, yh, 0), sibling)
    beside[0, 0, 1] = pass_on(half_block(0, yh, 1), sibling)
    for k in (2, 1, 3):
        along_x[k] = pass_on(quarter(0, yh, yl), place(plus(x, k, NX), yh, c, z, yl))

    loads[0].wait()
    loads[6].wait()

    def squares(j, total):
        part = xv[:, pl.ds(pl.multiple_of(j * PAIR, HD), PAIR)].astype(F32)
        return total + lane_tiles(part * part)

    total = lax.fori_loop(0, BLOCKS, squares, jnp.zeros((ROWS, HD), F32))
    inverse = lax.rsqrt(jnp.sum(total, axis=1, keepdims=True) * (1.0 / D) + 1e-06)
    inv_ref[...] = jnp.broadcast_to(inverse, (ROWS, HD))

    def normalise(j, carry):
        columns = pl.ds(pl.multiple_of(j * PAIR, HD), PAIR)
        normed = xv[:, columns].astype(F32) * inv_ref[:, :1]
        hid[j] = (normed * gain_ref[:, columns]).astype(BF16)
        return carry

    lax.fori_loop(0, BLOCKS, normalise, 0)

    def send_hidden(first, width):
        columns = pl.ds(first, width)
        copies = []
        for dx, dc in near:
            to_x, to_c = plus(x, dx, NX), plus(c, dc, 2)
            src, dst = hid.at[to_x * 2 + to_c, :, columns], xh.at[me, :, columns]
            copies.append(send(src, dst, place(to_x, yh, to_c, z, yl)))
        return copies

    hidden_a = send_hidden(0, WIDE)
    xh[me] = hid[me]

    for copy in loads[1:6]:
        copy.wait()
    doc_row = jnp.broadcast_to(doc_ref[...].astype(F32), (ROWS, ROWS))
    positions = lax.broadcasted_iota(jnp.int32, (ROWS, ROWS), 0)
    key_positions = lax.broadcasted_iota(jnp.int32, (ROWS, ROWS), 1)
    allowed = (positions >= key_positions) & (doc_row == doc_row.T)

    def stacked(ref, g):
        heads = range(g * PER_GROUP, (g + 1) * PER_GROUP)
        return jnp.concatenate([ref[:, h * HD : (h + 1) * HD] for h in heads], axis=0)

    for g in range(GROUPS):
        group = slice(g * HD, (g + 1) * HD)
        scores = dot(stacked(qv, g), kv[:, group], ((1,), (1,))) * (1.0 / math.sqrt(HD))
        scores = jnp.where(allowed[None], scores.reshape(PER_GROUP, ROWS, ROWS), -1e30)
        exponent = jnp.exp(scores - jnp.max(scores, axis=-1, keepdims=True))
        chances = exponent / jnp.sum(exponent, axis=-1, keepdims=True)
        chances = chances.reshape(PER_GROUP * ROWS, ROWS).astype(BF16)
        prob[g] = chances
        value_grad = dot(chances, stacked(gov, g), ((0,), (0,)))
        vgb[:, group] = value_grad.astype(BF16)
        vt[group, pl.ds(pl.multiple_of(me * HD, HD), HD)] = value_grad.T.astype(BF16)

    def turned(x, c):
        return vt.at[:, pl.ds(pl.multiple_of((x * 2 + c) * HD, HD), HD)]

    turned_x = {}
    for k in (2, 1, 3):
        turned_x[k] = pass_on(turned(x, c), place(plus(x, k, NX), yh, c, z, yl))
    turned_beside = [pass_on(turned(x, c), sibling)]
    relay()

    for i in (1, 2):
        along_y[0, i].wait_recv()
    spread_z(0, 1, True)
    relay()
    for k in (1, 3, 2):
        along_x[k].wait_recv()
        spread_y(k)
    relay()
    spread_beside(0, 1)
    relay()
    for copy in hidden_a:
        copy.wait_recv()
    hidden_b = send_hidden(WIDE, PAIR - WIDE)
    for k in (1, 3, 2):
        for i in range(3):
            along_y[k, i].wait_recv()
        spread_z(k, 0, k != 3)
        spread_z(k, 1, k == 3)
    relay()

    for k in (1, 3, 2):
        turned_x[k].wait_recv()
        turned_beside.append(pass_on(turned(plus(x, NX - k, NX), c), sibling))
    relay()

    def product(first, width):
        def step(i, carry):
            rows = pl.ds(pl.multiple_of(i * 256, 256), 256)
            columns = slice(first, first + width)
            part = dot(vt[rows, :], xh[:, :, columns].reshape(8 * ROWS, width), ((1,), (0,)))
            part = part.astype(BF16).reshape(8, 2, COLUMNS, width)
            to = pl.ds(pl.multiple_of(i * 128, 128), 128)
            pt[0, to, columns] = part[:, 0].reshape(128, width)
            pt[1, to, columns] = part[:, 1].reshape(128, width)
            return carry

        lax.fori_loop(0, 2, step, 0)

    parts = ((0, WIDE), (WIDE, PAIR - WIDE))
    y_sent, y_received = take(4), used[0] - 4
    crossing = []

    def send_y(to_c):
        first, width = parts[to_c]
        for side in (0, 1):
            to_y = 2 * c + side
            src, dst = pt.at[side, :, pl.ds(first, width)], yr.at[y, :, pl.ds(0, width)]
            mine = (to_y == y) & (c == to_c)
            there = remote(src, dst, on_y(to_y, to_c), y_sent + side * 2 + to_c, y_received + y)
            here = pltpu.make_async_copy(src, dst, recv_sem.at[y_received + y])
            crossing.append((mine, there))

            @pl.when(mine)
            def _():
                here.start()

            @pl.when(jnp.logical_not(mine))
            def _():
                there.start()

    z_first = take(NZ - 1)

    def along_z_copies(width):
        copies = []
        for dz in FAR_FIRST:
            to_z = plus(z, dz, NZ)
            i = z_first + dz - 1
            src, dst = zs.at[to_z, :, pl.ds(0, width)], zr.at[z, :, pl.ds(0, width)]
            copies.append(remote(src, dst, place(x, yh, c, to_z, yl), i, i))
        return copies

    def sum_y(core):
        width = parts[core][1]
        for i in range(NY):
            arrived = yr.at[i, :, pl.ds(0, width)]
            pltpu.make_async_copy(arrived, arrived, recv_sem.at[y_received + i]).wait()
        over_y = yr[0, :, :width].astype(F32)
        for i in range(1, NY):
            over_y = over_y + yr[i, :, :width].astype(F32)
        zs[:, :, :width] = over_y.astype(BF16).reshape(NZ, COLUMNS, width)
        for copy in along_z_copies(width):
            copy.start()
        zr[z, :, :width] = zs[z, :, :width]

    def sum_z(core):
        width = parts[core][1]
        for copy in along_z_copies(width):
            copy.wait()
        over_z = zr[0, :, :width].astype(F32)
        for i in range(1, NZ):
            over_z = over_z + zr[i, :, :width].astype(F32)
        return over_z * (1.0 / N_DP)

    middle = take(1)

    def middle_copy():
        return remote(middle_own, middle_in, sibling, middle, middle)

    for copy in turned_beside:
        copy.wait_recv()
    product(0, WIDE)
    send_y(0)
    relay()

    for key in ((0, 0, 0), (0, 0, 1), (1, 0, 0), (1, 0, 1)):
        beside.pop(key).wait_recv()
    ones = jnp.ones((8, 8 * ROWS), BF16)
    one_head = pl.ds(pl.multiple_of(x * HD, HD), HD)
    sz_own[:, PAIR:] = dot(ones, vt[one_head, :], ((1,), (1,)))[:1]

    def weighted(first, width):
        lanes = slice(first, first + width)

        def step(i, total):
            columns = pl.ds(pl.multiple_of(i * 128, 128), 128)
            turned_w = wf[x, c, :, :, :, columns].reshape(PAIR, 128)[lanes].astype(F32).T
            turned_w = turned_w.reshape(4, 2, COLUMNS, width)
            rows = pl.ds(pl.multiple_of(i * 64, 64), 64)
            for side in (0, 1):
                both = pt[side, rows, lanes].astype(F32) * turned_w[:, side].reshape(64, width)
                total = total + jnp.sum(both, axis=0, keepdims=True)
            return total

        total = lax.fori_loop(0, 4, step, jnp.zeros((1, width), F32))
        own = pl.ds(pl.multiple_of(me * PAIR + first, HD), width)
        sz_own[:, lanes] = total / gain_ref[:, own]

    weighted(0, WIDE)

    for copy in hidden_b:
        copy.wait_recv()
    product(WIDE, PAIR - WIDE)
    send_y(1)
    weighted(WIDE, PAIR - WIDE)
    small_z = []
    for dz in FAR_FIRST:
        small_z.append(send(sz_own, sz.at[z], place(x, yh, c, plus(z, dz, NZ), yl)))
    sz[z] = sz_own[...]
    pl.when(c == 0)(lambda: sum_y(0))

    for k in (1, 3, 2):
        spread_beside(k, 0)
        spread_beside(k, 1)

    def with_block(i, row_sum):
        from_x, from_y = plus(x, NX - lax.div(i, 2), NX), plus(yh, lax.rem(i, 2), 2)
        j = from_x * 2 + from_y
        columns = pl.ds(pl.multiple_of(j * PAIR, HD), PAIR)
        weights = wf[from_x, from_y].reshape(PAIR, KV)
        value[...] += dot(hid[j], weights, ((1,), (0,)))
        back = dot(vgb[...], weights, ((1,), (1,))).astype(BF16)
        hgrad[j] = back
        wide = back.astype(F32) * (xv[:, columns].astype(F32) * inv_ref[:, :1])
        return row_sum + lane_tiles(wide * gain_ref[:, columns])

    value[...] = jnp.zeros_like(value)
    row_sum = lax.fori_loop(0, 2, with_block, jnp.zeros((ROWS, HD), F32))

    pl.when(c == 1)(lambda: sum_y(1))

    for copy in beside.values():
        copy.wait_recv()
    row_sum = lax.fori_loop(2, BLOCKS, with_block, row_sum)

    value_b = (value[...] + bias_ref[...]).astype(BF16)
    for g in range(GROUPS):
        mixed = dot(prob[g], value_b[:, g * HD : (g + 1) * HD], ((1,), (0,))).astype(BF16)
        for i in range(PER_GROUP):
            h = g * PER_GROUP + i
            att[:, h * HD : (h + 1) * HD] = mixed[i * ROWS : (i + 1) * ROWS]

    for copy in small_z:
        copy.wait_recv()
    sg_own[...] = jnp.sum(sz[...], axis=0) * (1.0 / N_DP)
    gathered = []
    for dy in (2, 1, 3, 0):
        for dx, dc in near + [(0, 0)]:
            if (dx, dy, dc) != (0, 0, 0):
                to_y = plus(y, dy, NY)
                to = place(
                    plus(x, dx, NX), lax.div(to_y, 2), plus(c, dc, 2), z, lax.rem(to_y, 2)
                )
                gathered.append(send(sg_own, sg.at[y * 8 + me], to))
    sg[y * 8 + me] = sg_own[...]

    mean = jnp.sum(row_sum, axis=1, keepdims=True) * (1.0 / D)

    def inputs_gradient(j, carry):
        columns = pl.ds(pl.multiple_of(j * PAIR, HD), PAIR)
        inverse = inv_ref[:, :1]
        normed = xv[:, columns].astype(F32) * inverse
        scaled = hgrad[j].astype(F32) * gain_ref[:, columns]
        gi[:, columns] = (inverse * (scaled - normed * mean)).astype(BF16)
        return carry

    lax.fori_loop(0, BLOCKS, inputs_gradient, 0)

    @pl.when(c == 0)
    def _():
        over_z = sum_z(0)
        gw_ref[...] = over_z[:, :SHARE]
        middle_own[...] = over_z[:, WIDE - HD :]
        middle_copy().start()


    @pl.when(c == 1)
    def _():
        over_z = sum_z(1)
        middle_copy().wait_recv()
        gw_ref[...] = jnp.concatenate([middle_in[:, HD // 2 :], over_z], axis=1)

    for copy in gathered:
        copy.wait_recv()
    over_all = jnp.sum(sg[...].reshape(NY, 8, 1, SMALL), axis=0)
    gg_ref[...] = over_all[:, :, :PAIR]
    for i in range(NX):
        gb_ref[:, i * HD : (i + 1) * HD] = over_all[2 * i, :, PAIR:]

    for copy in sent:
        copy.wait_send()

    @pl.when(c == 0)
    def _():
        middle_copy().wait_send()

    for mine, there in crossing:

        @pl.when(jnp.logical_not(mine))
        def _():
            there.wait_send()


def hand_over(*refs):
    results, outs, sem = refs[:5], refs[5:10], refs[10]
    copies = [pltpu.make_async_copy(results[i], outs[i], sem.at[i]) for i in range(5)]
    for copy in copies:
        copy.start()
    for copy in copies:
        copy.wait()


def local(inputs, queries, keys, doc_ids, grad_out, gain, bias, w_value):
    whole = pl.BlockSpec(memory_space=pltpu.VMEM)
    anywhere = pl.BlockSpec(memory_space=pl.ANY)
    arguments = (
        inputs, queries, keys, grad_out, doc_ids.reshape(1, ROWS), gain.reshape(1, D),
        bias.reshape(1, KV), w_value,
    )
    summed = pl.pallas_call(
        kernel,
        out_shape=(
            pltpu.VMEM((ROWS, QD), BF16),
            pltpu.VMEM((ROWS, D), BF16),
            pltpu.VMEM((COLUMNS, SHARE), F32),
            pltpu.VMEM((BLOCKS, 1, PAIR), F32),
            pltpu.VMEM((1, KV), F32),
        ),
        in_specs=[anywhere] * len(arguments),
        out_specs=(whole,) * 5,
        scratch_shapes=[
            pltpu.VMEM((ROWS, D), BF16),
            pltpu.VMEM((ROWS, QD), BF16),
            pltpu.VMEM((ROWS, KV), BF16),
            pltpu.VMEM((ROWS, QD), BF16),
            pltpu.VMEM((1, ROWS), jnp.int32),
            pltpu.VMEM((1, D), F32),
            pltpu.VMEM((1, KV), F32),
            pltpu.VMEM((BLOCKS, ROWS, PAIR), BF16),
            pltpu.VMEM((ROWS, HD), F32),
            pltpu.VMEM((GROUPS, PER_GROUP * ROWS, ROWS), BF16),
            pltpu.VMEM((ROWS, KV), BF16),
            pltpu.VMEM((KV, 8 * ROWS), BF16),
            pltpu.VMEM((NX, 2, 2, 4, QUARTER, KV), BF16),
            pltpu.VMEM((8, ROWS, PAIR), BF16),
            pltpu.VMEM((ROWS, KV), F32),
            pltpu.VMEM((BLOCKS, ROWS, PAIR), BF16),
            pltpu.VMEM((2, KV // 2, PAIR), BF16),
            pltpu.VMEM((NY, KV // 2, WIDE), BF16),
            pltpu.VMEM((NZ, COLUMNS, WIDE), BF16),
            pltpu.VMEM((NZ, COLUMNS, WIDE), BF16),
            pltpu.VMEM((COLUMNS, HD), F32),
            pltpu.VMEM((COLUMNS, HD), F32),
            pltpu.VMEM((1, SMALL), F32),
            pltpu.VMEM((NZ, 1, SMALL), F32),
            pltpu.VMEM((1, SMALL), F32),
            pltpu.VMEM((8 * NY, 1, SMALL), F32),
            pltpu.SemaphoreType.DMA((11,)),
            pltpu.SemaphoreType.DMA((COPIES,)),
            pltpu.SemaphoreType.DMA((COPIES,)),
            pltpu.SemaphoreType.REGULAR,
            pltpu.SemaphoreType.REGULAR,
        ],
        compiler_params=pltpu.CompilerParams(
            collective_id=0, has_side_effects=True, vmem_limit_bytes=32 * 1024 * 1024
        ),
    )(
        *(pltpu.with_memory_space_constraint(argument, pltpu.HBM) for argument in arguments)
    )
    attention, grad_inputs, grad_w, grad_gain, grad_bias = pl.pallas_call(
        hand_over,
        out_shape=(
            jax.ShapeDtypeStruct((ROWS, QD), BF16),
            jax.ShapeDtypeStruct((ROWS, D), BF16),
            jax.ShapeDtypeStruct((COLUMNS, SHARE), F32),
            jax.ShapeDtypeStruct((BLOCKS, 1, PAIR), F32),
            jax.ShapeDtypeStruct((1, KV), F32),
        ),
        in_specs=[whole] * 5,
        out_specs=(anywhere,) * 5,
        scratch_shapes=[pltpu.SemaphoreType.DMA((5,))],
        compiler_params=pltpu.CompilerParams(vmem_limit_bytes=16 * 1024 * 1024),
    )(*summed)
    return attention, grad_inputs, grad_w.T, grad_gain.reshape(D), grad_bias.reshape(KV)


def solution(mesh):
    placed = (
        P(("blk", "dp"), None),
        P(("blk", "dp"), None),
        P(("blk", "dp"), None),
        P(("blk", "dp")),
        P(("blk", "dp"), None),
        P(),
        P(),
        P("blk", None),
    )
    return jax.shard_map(
        local,
        mesh=mesh,
        in_specs=placed,
        out_specs=(P(("blk", "dp"), None), P(("blk", "dp"), None), P("blk", "dp"), P(), P()),
        check_vma=False,
    )
```

```python
import math

import jax
import jax.numpy as jnp
from jax import lax
from jax.experimental import pallas as pl
from jax.experimental.pallas import tpu as pltpu
from jax.sharding import PartitionSpec as P

MESH = pl.DeviceIdType.MESH
F32, BF16 = jnp.float32, jnp.bfloat16

D = 5120
HD = 128
ROWS = 128
GROUPS = 4
PER_GROUP = 5
KV = GROUPS * HD
QD = KV * PER_GROUP
NX, NY, NZ = 4, 4, 16
SHARE = 320
QUARTER = SHARE // 4
PAIR = 2 * SHARE
BLOCKS = D // PAIR
WIDE = 384
COLUMNS = 16
SMALL = PAIR + HD
N_DP = 32
COPIES = 144
FAR_FIRST = (8, 7, 9, 6, 10, 5, 11, 4, 12, 3, 13, 2, 14, 1, 15)


def dot(a, b, dims):
    return lax.dot_general(a, b, (dims, ((), ())), preferred_element_type=F32)


def lane_tiles(a):
    total = a[:, :HD]
    for i in range(1, a.shape[1] // HD):
        total = total + a[:, i * HD : (i + 1) * HD]
    return total


def kernel(
    x_any, q_any, k_any, go_any, doc_any, gain_any, bias_any, w_any,
    att, gi, gw_ref, gg_ref, gb_ref,
    xv, qv, kv, gov, doc_ref, gain_ref, bias_ref, hid, inv_ref, prob, vgb, vt, wf, xh, value,
    hgrad, pt, yr, zs, zr, middle_own, middle_in, sz_own, sz, sg_own, sg,
    local_sem, send_sem, recv_sem, lower_sem, upper_sem,
):
    blk, dp = lax.axis_index("blk"), lax.axis_index("dp")
    x, yh, c = lax.div(blk, 4), lax.rem(lax.div(blk, 2), 2), lax.rem(blk, 2)
    z, yl = lax.div(dp, 2), lax.rem(dp, 2)
    y, half = yh * 2 + yl, lax.rem(z, 2)
    me = x * 2 + c

    def place(x, yh, c, z, yl):
        return (x * 4 + yh * 2 + c, z * 2 + yl)

    def on_y(y, c):
        return place(x, lax.div(y, 2), c, z, lax.rem(y, 2))

    def plus(a, by, n):
        return lax.rem(a + by, n)

    used = [0]

    def take(n):
        used[0] += n
        return used[0] - n

    def remote(src, dst, to, sent_at, received_at):
        return pltpu.make_async_remote_copy(
            src_ref=src,
            dst_ref=dst,
            send_sem=send_sem.at[sent_at],
            recv_sem=recv_sem.at[received_at],
            device_id=to,
            device_id_type=MESH,
        )

    sent = []

    def send(src, dst, to):
        i = take(1)
        copy = remote(src, dst, to, i, i)
        copy.start()
        sent.append(copy)
        return copy

    def pass_on(ref, to):
        return send(ref, ref, to)

    loads = [
        pltpu.make_async_copy(x_any, xv, local_sem.at[0]),
        pltpu.make_async_copy(q_any, qv, local_sem.at[1]),
        pltpu.make_async_copy(k_any, kv, local_sem.at[2]),
        pltpu.make_async_copy(go_any, gov, local_sem.at[3]),
        pltpu.make_async_copy(doc_any, doc_ref, local_sem.at[8]),
        pltpu.make_async_copy(bias_any, bias_ref, local_sem.at[9]),
        pltpu.make_async_copy(gain_any, gain_ref, local_sem.at[10]),
    ]
    loads += [
        pltpu.make_async_copy(
            w_any.at[pl.ds(i * QUARTER, QUARTER)], wf.at[x, yh, c, i], local_sem.at[4 + i]
        )
        for i in range(4)
    ]
    for copy in loads:
        copy.start()

    near = [(dx, dc) for dx in (1, 3, 2, 0) for dc in (0, 1) if (dx, dc) != (0, 0)]
    sibling = place(x, yh, 1 - c, z, yl)
    up = place(x, yh, c, plus(z, 1, NZ), yl)
    down = place(x, yh, c, plus(z, NZ - 1, NZ), yl)

    barrier = pltpu.get_barrier_semaphore()
    partners = [place(plus(x, dx, NX), yh, plus(c, dc, 2), z, yl) for dx, dc in near]
    partners += [on_y(plus(y, dy, NY), plus(c, dc, 2)) for dy in (1, 2, 3) for dc in (0, 1)]
    partners += [up, down]
    for partner in partners:
        pl.semaphore_signal(barrier, inc=1, device_id=partner, device_id_type=MESH)

    pl.semaphore_wait(barrier, len(partners))

    rounds = [0]

    def relay():
        if rounds[0] > 0:
            pl.semaphore_wait(lower_sem, 1)
            pl.semaphore_wait(upper_sem, 1)
        if rounds[0] < NZ // 2 - 1:
            pl.semaphore_signal(lower_sem, inc=1, device_id=up, device_id_type=MESH)
            pl.semaphore_signal(upper_sem, inc=1, device_id=down, device_id_type=MESH)
        rounds[0] += 1

    relay()

    def quarter(k, y_hi, y_lo):
        return wf.at[plus(x, NX - k, NX), y_hi, c, half * 2 + y_lo]

    def half_block(k, y_hi, h):
        return wf.at[plus(x, NX - k, NX), y_hi, c, pl.ds(h * 2, 2)]

    for copy in loads[7:]:
        copy.wait()
    along_x, along_y, along_z, beside = {}, {}, {}, {}

    others = (
        place(x, yh, c, z, 1 - yl),
        place(x, 1 - yh, c, z, yl),
        place(x, 1 - yh, c, z, 1 - yl),
    )

    def spread_y(k):
        for i in range(1 if k == 0 else 0, 3):
            along_y[k, i] = pass_on(quarter(k, yh, yl), others[i])

    def spread_z(k, other, is_up):
        y_hi = 1 - yh if other else yh
        along_z[other, k] = pass_on(half_block(k, y_hi, half), up if is_up else down)
        beside[other, k, 0] = pass_on(half_block(k, y_hi, half), sibling)

    def spread_beside(k, other):
        along_z[other, k].wait_recv()
        y_hi = 1 - yh if other else yh
        beside[other, k, 1] = pass_on(half_block(k, y_hi, 1 - half), sibling)

    spread_y(0)
    beside[0, 0, 0] = pass_on(half_block(0, yh, 0), sibling)
    beside[0, 0, 1] = pass_on(half_block(0, yh, 1), sibling)
    for k in (2, 1, 3):
        along_x[k] = pass_on(quarter(0, yh, yl), place(plus(x, k, NX), yh, c, z, yl))

    loads[0].wait()
    loads[6].wait()

    def squares(j, total):
        part = xv[:, pl.ds(pl.multiple_of(j * PAIR, HD), PAIR)].astype(F32)
        return total + lane_tiles(part * part)

    total = lax.fori_loop(0, BLOCKS, squares, jnp.zeros((ROWS, HD), F32))
    inverse = lax.rsqrt(jnp.sum(total, axis=1, keepdims=True) * (1.0 / D) + 1e-06)
    inv_ref[...] = jnp.broadcast_to(inverse, (ROWS, HD))

    def normalise(j, carry):
        columns = pl.ds(pl.multiple_of(j * PAIR, HD), PAIR)
        normed = xv[:, columns].astype(F32) * inv_ref[:, :1]
        hid[j] = (normed * gain_ref[:, columns]).astype(BF16)
        return carry


    def send_hidden(first, width, fresh):
        columns = pl.ds(first, width)
        copies = []
        for dx, dc in near:
            to_x, to_c = plus(x, dx, NX), plus(c, dc, 2)
            if fresh:
                normalise(to_x * 2 + to_c, 0)
            src, dst = hid.at[to_x * 2 + to_c, :, columns], xh.at[me, :, columns]
            copies.append(send(src, dst, place(to_x, yh, to_c, z, yl)))
        return copies

    hidden_a = send_hidden(0, WIDE, True)
    normalise(me, 0)
    xh[me] = hid[me]

    for copy in loads[1:6]:
        copy.wait()
    doc_row = jnp.broadcast_to(doc_ref[...].astype(F32), (ROWS, ROWS))
    positions = lax.broadcasted_iota(jnp.int32, (ROWS, ROWS), 0)
    key_positions = lax.broadcasted_iota(jnp.int32, (ROWS, ROWS), 1)
    allowed = (positions >= key_positions) & (doc_row == doc_row.T)

    def stacked(ref, g):
        heads = range(g * PER_GROUP, (g + 1) * PER_GROUP)
        return jnp.concatenate([ref[:, h * HD : (h + 1) * HD] for h in heads], axis=0)

    for g in range(GROUPS):
        group = slice(g * HD, (g + 1) * HD)
        scores = dot(stacked(qv, g), kv[:, group], ((1,), (1,))) * (1.0 / math.sqrt(HD))
        scores = jnp.where(allowed[None], scores.reshape(PER_GROUP, ROWS, ROWS), -1e30)
        exponent = jnp.exp(scores - jnp.max(scores, axis=-1, keepdims=True))
        chances = exponent / jnp.sum(exponent, axis=-1, keepdims=True)
        chances = chances.reshape(PER_GROUP * ROWS, ROWS).astype(BF16)
        prob[g] = chances
        value_grad = dot(chances, stacked(gov, g), ((0,), (0,)))
        vgb[:, group] = value_grad.astype(BF16)
        vt[group, pl.ds(pl.multiple_of(me * HD, HD), HD)] = value_grad.T.astype(BF16)

    def turned(x, c):
        return vt.at[:, pl.ds(pl.multiple_of((x * 2 + c) * HD, HD), HD)]

    turned_x = {}
    for k in (2, 1, 3):
        turned_x[k] = pass_on(turned(x, c), place(plus(x, k, NX), yh, c, z, yl))
    turned_beside = [pass_on(turned(x, c), sibling)]
    relay()

    for i in (1, 2):
        along_y[0, i].wait_recv()
    spread_z(0, 1, True)
    relay()
    for k in (1, 3, 2):
        along_x[k].wait_recv()
        spread_y(k)
    relay()
    spread_beside(0, 1)
    relay()
    for copy in hidden_a:
        copy.wait_recv()
    hidden_b = send_hidden(WIDE, PAIR - WIDE, False)
    for k in (1, 3, 2):
        for i in range(3):
            along_y[k, i].wait_recv()
        spread_z(k, 0, k != 3)
        spread_z(k, 1, k == 3)
    relay()

    for k in (1, 3, 2):
        turned_x[k].wait_recv()
        turned_beside.append(pass_on(turned(plus(x, NX - k, NX), c), sibling))
    relay()

    def product(first, width):
        def step(i, carry):
            rows = pl.ds(pl.multiple_of(i * 256, 256), 256)
            columns = slice(first, first + width)
            part = dot(vt[rows, :], xh[:, :, columns].reshape(8 * ROWS, width), ((1,), (0,)))
            part = part.astype(BF16).reshape(8, 2, COLUMNS, width)
            to = pl.ds(pl.multiple_of(i * 128, 128), 128)
            pt[0, to, columns] = part[:, 0].reshape(128, width)
            pt[1, to, columns] = part[:, 1].reshape(128, width)
            return carry

        lax.fori_loop(0, 2, step, 0)

    parts = ((0, WIDE), (WIDE, PAIR - WIDE))
    y_sent, y_received = take(4), used[0] - 4
    crossing = []

    def send_y(to_c):
        first, width = parts[to_c]
        for side in (0, 1):
            to_y = 2 * c + side
            src, dst = pt.at[side, :, pl.ds(first, width)], yr.at[y, :, pl.ds(0, width)]
            mine = (to_y == y) & (c == to_c)
            there = remote(src, dst, on_y(to_y, to_c), y_sent + side * 2 + to_c, y_received + y)
            here = pltpu.make_async_copy(src, dst, recv_sem.at[y_received + y])
            crossing.append((mine, there))

            @pl.when(mine)
            def _():
                here.start()

            @pl.when(jnp.logical_not(mine))
            def _():
                there.start()

    z_first = take(NZ - 1)

    def along_z_copies(width):
        copies = []
        for dz in FAR_FIRST:
            to_z = plus(z, dz, NZ)
            i = z_first + dz - 1
            src, dst = zs.at[to_z, :, pl.ds(0, width)], zr.at[z, :, pl.ds(0, width)]
            copies.append(remote(src, dst, place(x, yh, c, to_z, yl), i, i))
        return copies

    def sum_y(core):
        width = parts[core][1]
        for i in range(NY):
            arrived = yr.at[i, :, pl.ds(0, width)]
            pltpu.make_async_copy(arrived, arrived, recv_sem.at[y_received + i]).wait()
        over_y = yr[0, :, :width].astype(F32)
        for i in range(1, NY):
            over_y = over_y + yr[i, :, :width].astype(F32)
        zs[:, :, :width] = over_y.astype(BF16).reshape(NZ, COLUMNS, width)
        for copy in along_z_copies(width):
            copy.start()
        zr[z, :, :width] = zs[z, :, :width]

    def sum_z(core):
        width = parts[core][1]
        for copy in along_z_copies(width):
            copy.wait()
        over_z = zr[0, :, :width].astype(F32)
        for i in range(1, NZ):
            over_z = over_z + zr[i, :, :width].astype(F32)
        return over_z * (1.0 / N_DP)

    middle = take(1)

    def middle_copy():
        return remote(middle_own, middle_in, sibling, middle, middle)

    for copy in turned_beside:
        copy.wait_recv()
    product(0, WIDE)
    send_y(0)
    relay()

    for key in ((0, 0, 0), (0, 0, 1), (1, 0, 0), (1, 0, 1)):
        beside.pop(key).wait_recv()
    ones = jnp.ones((8, 8 * ROWS), BF16)
    one_head = pl.ds(pl.multiple_of(x * HD, HD), HD)
    sz_own[:, PAIR:] = dot(ones, vt[one_head, :], ((1,), (1,)))[:1]

    def weighted(first, width):
        lanes = slice(first, first + width)

        def step(i, total):
            columns = pl.ds(pl.multiple_of(i * 128, 128), 128)
            turned_w = wf[x, c, :, :, :, columns].reshape(PAIR, 128)[lanes].astype(F32).T
            turned_w = turned_w.reshape(4, 2, COLUMNS, width)
            rows = pl.ds(pl.multiple_of(i * 64, 64), 64)
            for side in (0, 1):
                both = pt[side, rows, lanes].astype(F32) * turned_w[:, side].reshape(64, width)
                total = total + jnp.sum(both, axis=0, keepdims=True)
            return total

        total = lax.fori_loop(0, 4, step, jnp.zeros((1, width), F32))
        own = pl.ds(pl.multiple_of(me * PAIR + first, HD), width)
        sz_own[:, lanes] = total / gain_ref[:, own]

    weighted(0, WIDE)

    for copy in hidden_b:
        copy.wait_recv()
    product(WIDE, PAIR - WIDE)
    send_y(1)
    weighted(WIDE, PAIR - WIDE)
    small_z = []
    for dz in FAR_FIRST:
        small_z.append(send(sz_own, sz.at[z], place(x, yh, c, plus(z, dz, NZ), yl)))
    sz[z] = sz_own[...]
    pl.when(c == 0)(lambda: sum_y(0))

    for k in (1, 3, 2):
        spread_beside(k, 0)
        spread_beside(k, 1)

    def with_block(i, row_sum):
        from_x, from_y = plus(x, NX - lax.div(i, 2), NX), plus(yh, lax.rem(i, 2), 2)
        j = from_x * 2 + from_y
        columns = pl.ds(pl.multiple_of(j * PAIR, HD), PAIR)
        weights = wf[from_x, from_y].reshape(PAIR, KV)
        value[...] += dot(hid[j], weights, ((1,), (0,)))
        back = dot(vgb[...], weights, ((1,), (1,))).astype(BF16)
        hgrad[j] = back
        wide = back.astype(F32) * (xv[:, columns].astype(F32) * inv_ref[:, :1])
        return row_sum + lane_tiles(wide * gain_ref[:, columns])

    value[...] = jnp.zeros_like(value)
    row_sum = lax.fori_loop(0, 2, with_block, jnp.zeros((ROWS, HD), F32))

    pl.when(c == 1)(lambda: sum_y(1))

    for copy in beside.values():
        copy.wait_recv()
    row_sum = lax.fori_loop(2, BLOCKS, with_block, row_sum)

    value_b = (value[...] + bias_ref[...]).astype(BF16)
    for g in range(GROUPS):
        mixed = dot(prob[g], value_b[:, g * HD : (g + 1) * HD], ((1,), (0,))).astype(BF16)
        for i in range(PER_GROUP):
            h = g * PER_GROUP + i
            att[:, h * HD : (h + 1) * HD] = mixed[i * ROWS : (i + 1) * ROWS]

    for copy in small_z:
        copy.wait_recv()
    sg_own[...] = jnp.sum(sz[...], axis=0) * (1.0 / N_DP)
    gathered = []
    for dy in (2, 1, 3, 0):
        for dx, dc in near + [(0, 0)]:
            if (dx, dy, dc) != (0, 0, 0):
                to_y = plus(y, dy, NY)
                to = place(
                    plus(x, dx, NX), lax.div(to_y, 2), plus(c, dc, 2), z, lax.rem(to_y, 2)
                )
                gathered.append(send(sg_own, sg.at[y * 8 + me], to))
    sg[y * 8 + me] = sg_own[...]

    mean = jnp.sum(row_sum, axis=1, keepdims=True) * (1.0 / D)

    def inputs_gradient(j, carry):
        columns = pl.ds(pl.multiple_of(j * PAIR, HD), PAIR)
        inverse = inv_ref[:, :1]
        normed = xv[:, columns].astype(F32) * inverse
        scaled = hgrad[j].astype(F32) * gain_ref[:, columns]
        gi[:, columns] = (inverse * (scaled - normed * mean)).astype(BF16)
        return carry

    lax.fori_loop(0, BLOCKS, inputs_gradient, 0)

    @pl.when(c == 0)
    def _():
        over_z = sum_z(0)
        gw_ref[...] = over_z[:, :SHARE]
        middle_own[...] = over_z[:, WIDE - HD :]
        middle_copy().start()


    @pl.when(c == 1)
    def _():
        over_z = sum_z(1)
        middle_copy().wait_recv()
        gw_ref[...] = jnp.concatenate([middle_in[:, HD // 2 :], over_z], axis=1)

    for copy in gathered:
        copy.wait_recv()
    over_all = jnp.sum(sg[...].reshape(NY, 8, 1, SMALL), axis=0)
    gg_ref[...] = over_all[:, :, :PAIR]
    for i in range(NX):
        gb_ref[:, i * HD : (i + 1) * HD] = over_all[2 * i, :, PAIR:]

    for copy in sent:
        copy.wait_send()

    @pl.when(c == 0)
    def _():
        middle_copy().wait_send()

    for mine, there in crossing:

        @pl.when(jnp.logical_not(mine))
        def _():
            there.wait_send()


def hand_over(*refs):
    results, outs, sem = refs[:5], refs[5:10], refs[10]
    copies = [pltpu.make_async_copy(results[i], outs[i], sem.at[i]) for i in range(5)]
    for copy in copies:
        copy.start()
    for copy in copies:
        copy.wait()


def local(inputs, queries, keys, doc_ids, grad_out, gain, bias, w_value):
    whole = pl.BlockSpec(memory_space=pltpu.VMEM)
    anywhere = pl.BlockSpec(memory_space=pl.ANY)
    arguments = (
        inputs, queries, keys, grad_out, doc_ids.reshape(1, ROWS), gain.reshape(1, D),
        bias.reshape(1, KV), w_value,
    )
    summed = pl.pallas_call(
        kernel,
        out_shape=(
            pltpu.VMEM((ROWS, QD), BF16),
            pltpu.VMEM((ROWS, D), BF16),
            pltpu.VMEM((COLUMNS, SHARE), F32),
            pltpu.VMEM((BLOCKS, 1, PAIR), F32),
            pltpu.VMEM((1, KV), F32),
        ),
        in_specs=[anywhere] * len(arguments),
        out_specs=(whole,) * 5,
        scratch_shapes=[
            pltpu.VMEM((ROWS, D), BF16),
            pltpu.VMEM((ROWS, QD), BF16),
            pltpu.VMEM((ROWS, KV), BF16),
            pltpu.VMEM((ROWS, QD), BF16),
            pltpu.VMEM((1, ROWS), jnp.int32),
            pltpu.VMEM((1, D), F32),
            pltpu.VMEM((1, KV), F32),
            pltpu.VMEM((BLOCKS, ROWS, PAIR), BF16),
            pltpu.VMEM((ROWS, HD), F32),
            pltpu.VMEM((GROUPS, PER_GROUP * ROWS, ROWS), BF16),
            pltpu.VMEM((ROWS, KV), BF16),
            pltpu.VMEM((KV, 8 * ROWS), BF16),
            pltpu.VMEM((NX, 2, 2, 4, QUARTER, KV), BF16),
            pltpu.VMEM((8, ROWS, PAIR), BF16),
            pltpu.VMEM((ROWS, KV), F32),
            pltpu.VMEM((BLOCKS, ROWS, PAIR), BF16),
            pltpu.VMEM((2, KV // 2, PAIR), BF16),
            pltpu.VMEM((NY, KV // 2, WIDE), BF16),
            pltpu.VMEM((NZ, COLUMNS, WIDE), BF16),
            pltpu.VMEM((NZ, COLUMNS, WIDE), BF16),
            pltpu.VMEM((COLUMNS, HD), F32),
            pltpu.VMEM((COLUMNS, HD), F32),
            pltpu.VMEM((1, SMALL), F32),
            pltpu.VMEM((NZ, 1, SMALL), F32),
            pltpu.VMEM((1, SMALL), F32),
            pltpu.VMEM((8 * NY, 1, SMALL), F32),
            pltpu.SemaphoreType.DMA((11,)),
            pltpu.SemaphoreType.DMA((COPIES,)),
            pltpu.SemaphoreType.DMA((COPIES,)),
            pltpu.SemaphoreType.REGULAR,
            pltpu.SemaphoreType.REGULAR,
        ],
        compiler_params=pltpu.CompilerParams(
            collective_id=0, has_side_effects=True, vmem_limit_bytes=32 * 1024 * 1024
        ),
    )(
        *(pltpu.with_memory_space_constraint(argument, pltpu.HBM) for argument in arguments)
    )
    attention, grad_inputs, grad_w, grad_gain, grad_bias = pl.pallas_call(
        hand_over,
        out_shape=(
            jax.ShapeDtypeStruct((ROWS, QD), BF16),
            jax.ShapeDtypeStruct((ROWS, D), BF16),
            jax.ShapeDtypeStruct((COLUMNS, SHARE), F32),
            jax.ShapeDtypeStruct((BLOCKS, 1, PAIR), F32),
            jax.ShapeDtypeStruct((1, KV), F32),
        ),
        in_specs=[whole] * 5,
        out_specs=(anywhere,) * 5,
        scratch_shapes=[pltpu.SemaphoreType.DMA((5,))],
        compiler_params=pltpu.CompilerParams(vmem_limit_bytes=16 * 1024 * 1024),
    )(*summed)
    return attention, grad_inputs, grad_w.T, grad_gain.reshape(D), grad_bias.reshape(KV)


def solution(mesh):
    placed = (
        P(("blk", "dp"), None),
        P(("blk", "dp"), None),
        P(("blk", "dp"), None),
        P(("blk", "dp")),
        P(("blk", "dp"), None),
        P(),
        P(),
        P("blk", None),
    )
    return jax.shard_map(
        local,
        mesh=mesh,
        in_specs=placed,
        out_specs=(P(("blk", "dp"), None), P(("blk", "dp"), None), P("blk", "dp"), P(), P()),
        check_vma=False,
    )
```
